32 devices in a mesh: ctx: 16 (over z, y, core), head: 2 (over x).
Axes of the slice: x: 2, y: 2, z: 4, core: 2. Of those that a mesh axis runs over, the one named last changes fastest.
Arguments:
- queries: bfloat16 [4096, 2048], P('ctx', 'head'), parts along dimension 1, may hold values from -4.6 to 4.6
- key_vectors: bfloat16 [4096, 256], P('ctx', 'head'), parts along dimension 1, may hold values from -4.6 to 4.6
- value_vectors: bfloat16 [4096, 256], P('ctx', 'head'), parts along dimension 1, may hold values from -6 to 6
- doc_ids: int32 [4096], replicated, may hold values from 0 to 9, never falling along the last dimension, each value on 1 to 768 neighbouring positions
- grad_out: bfloat16 [4096, 2048], P('ctx', 'head'), parts along dimension 1, may hold values from -6 to 6
Outputs:
- attended: bfloat16 [4096, 2048], P('ctx', 'head'), parts along dimension 1
- grad_query: bfloat16 [4096, 2048], P('ctx', 'head'), parts along dimension 1
- grad_key: bfloat16 [4096, 256], P('ctx', 'head'), parts along dimension 1
- grad_value: bfloat16 [4096, 256], P('ctx', 'head'), parts along dimension 1
The draws below stay inside these ranges and needn't reach their ends.
There are 2 independent parts, one for each index of `head`. The reference program is written for one: setup_inputs(seed, part) draws one part's arguments, and reference() takes and returns one part's arrays. A program takes and returns all parts, laid end to end along the dimension named above; an argument that names none is the same for every part. Nothing has to cross between parts.
Inputs may be any that keep to these rules, and one draw needn't show every extreme that they name: doc_ids never fall along the sequence; each document holds 1 to 768 positions and one holds exactly 768.
All inputs are finite; a program needn't handle non-finite values.
Results may differ from the reference program's by a relative error of at most 0.029.
Values may be sent and summed in bfloat16 or wider, within the bound.
No kernel may reach another device: no remote copies, remote signals or barrier semaphores. Data moves between devices by JAX's collectives and lax.ppermute only.
A program may use at most 64 MiB of HBM per device.

```python
import math
import jax
import jax.numpy as jnp
import numpy as np
from jax import lax

HD = 128
QH = 8
TOK_DEV = 256
REACH = 3
TOKENS = 4096
MOST = 768
DOCS = 10
N_CTX = 16


def draw_key_vectors(key, part):
    drawn = jnp.clip(jax.random.normal(jax.random.fold_in(key, 1), (TOKENS, HD), jnp.float32), -4.6, 4.6)
    return drawn.astype(jnp.bfloat16)


def draw_queries(key, part):
    drawn = jnp.clip(jax.random.normal(jax.random.fold_in(key, 2), (TOKENS, QH * HD), jnp.float32), -4.6, 4.6)
    return drawn.astype(jnp.bfloat16)


def level_of(stream_key, extent, cuts, smallest, high):
    def one(axis_at, parts):
        draws = jax.random.uniform(jax.random.fold_in(jax.random.fold_in(stream_key, 6), axis_at), (parts,), jnp.float32, smallest / len(cuts), high / len(cuts))
        return jnp.repeat(jnp.exp(draws), extent[axis_at] // parts).reshape((-1,) + (1,) * (len(extent) - axis_at - 1))

    loudness = one(*cuts[0])
    for cut in cuts[1:]:
        loudness = loudness * one(*cut)
    return loudness


def profile(count, total, most, slope):
    loads = [(1 << 20) // math.isqrt(grade ** slope) + 1 for grade in range(2, count + 1)]
    spare, counts = total - most - (count - 1), [1] * (count - 1)
    while spare > 0:
        candidates = [i for i in range(count - 1) if counts[i] < most]
        mass, left = sum([loads[i] for i in candidates]), spare
        for i in candidates:
            extra = min(most - counts[i], max(1, left * loads[i] // mass), spare)
            counts[i] = counts[i] + extra
            spare = spare - extra
    return np.array([most] + counts)


def uneven_parts(own_key, count, total, most, slope):
    if count == 2:
        one = jax.random.randint(own_key, (), max(1, total - most), min(most, total - 1) + 1)
        return jnp.stack([one, total - one])
    lengths = jnp.asarray(profile(count, total, most, slope), jnp.int32)
    couples = (count - 1) // 2
    giver, taker = lengths[1:1 + 2 * couples:2], lengths[2:2 + 2 * couples:2]
    margin = jnp.minimum(giver - 1, most - taker)
    shifted = jax.random.randint(jax.random.fold_in(own_key, 1), (couples,), 0, 1 << 20) % (margin + 1)
    lengths = lengths.at[1:1 + 2 * couples:2].set(giver - shifted).at[2:2 + 2 * couples:2].set(taker + shifted)
    return lengths[jax.random.permutation(jax.random.fold_in(own_key, 2), count)]


def noise(own_key, extent, scale, most, cuts=(), kind=jnp.bfloat16):
    array = scale * jax.random.normal(own_key, extent, jnp.float32)
    if cuts:
        array = array * level_of(own_key, extent, cuts, -0.22, 0.18)
    return jnp.clip(array, -most, most).astype(kind)


def setup_inputs(seed: int = 0, part: int = 0) -> dict:
    key_list = jax.random.split(jax.random.key(seed), 6)
    part_splits = jax.random.split(jax.random.fold_in(key_list[5], part), 6)
    return {
        "queries": draw_queries(jax.random.fold_in(jax.random.fold_in(key_list[5], part), 71), part),
        "key_vectors": draw_key_vectors(jax.random.fold_in(jax.random.fold_in(key_list[5], part), 71), part),
        "value_vectors": noise(part_splits[2], (TOKENS, HD), 1.0, 6.0, ((0, 16),)),
        "doc_ids": jnp.searchsorted(jnp.cumsum(uneven_parts(key_list[3], DOCS, TOKENS, MOST, 1)), jnp.arange(TOKENS), side="right").astype(jnp.int32),
        "grad_out": noise(part_splits[4], (TOKENS, QH * HD), 1.0, 6.0, ((0, 16),)),
    }


def block_grads(query_rows, grad_rows, key_value, query_pos, key_pos, query_doc, key_doc):
    row_count = query_rows.shape[0]
    head_dim = key_value.shape[1] // 2
    score_scale = head_dim ** -0.5
    query_heads = query_rows.astype(jnp.float32).reshape(row_count, -1, head_dim)
    grad_heads = grad_rows.astype(jnp.float32).reshape(row_count, -1, head_dim)
    key_part = key_value[:, :head_dim].astype(jnp.float32)
    value_part = key_value[:, head_dim:].astype(jnp.float32)
    allowed = (query_doc[:, None] == key_doc[None, :]) & (key_pos[None, :] <= query_pos[:, None]) & (key_pos[None, :] >= 0)
    scores = jnp.einsum("thd,kd->htk", query_heads, key_part) * score_scale
    scores = jnp.where(allowed[None], scores, -1e30)
    row_max = jnp.max(scores, axis=-1, keepdims=True)
    row_sum = jnp.sum(jnp.where(allowed[None], jnp.exp(scores - row_max), 0.0), axis=-1, keepdims=True)
    log_norm = row_max + jnp.log(row_sum)
    probs = jnp.where(allowed[None], jnp.exp(scores - log_norm), 0.0)
    weights = probs.astype(jnp.bfloat16).astype(jnp.float32)
    attended = jnp.einsum("htk,kd->thd", weights, value_part).astype(jnp.bfloat16)
    delta = jnp.sum(grad_heads * attended.astype(jnp.float32), axis=-1)
    grad_prob = jnp.einsum("thd,kd->htk", grad_heads, value_part)
    dscore = (probs * (grad_prob - jnp.transpose(delta)[:, :, None])).astype(jnp.bfloat16).astype(jnp.float32)
    grad_query = (jnp.einsum("htk,kd->thd", dscore, key_part) * score_scale).astype(jnp.bfloat16)
    grad_key = jnp.einsum("htk,thd->kd", dscore, query_heads) * score_scale
    grad_value = jnp.einsum("htk,thd->kd", weights, grad_heads)
    return attended.reshape(row_count, -1), grad_query.reshape(row_count, -1), jnp.concatenate([grad_key, grad_value], axis=1)


def reference(queries, key_vectors, value_vectors, doc_ids, grad_out):
    row_count = TOK_DEV
    key_span = (REACH + 1) * row_count
    key_value = jnp.concatenate([key_vectors, value_vectors], axis=1)
    padded_kv = jnp.concatenate([jnp.zeros((REACH * row_count, 2 * HD), jnp.bfloat16), key_value], axis=0)
    padded_doc = jnp.concatenate([jnp.full((REACH * row_count,), -1, jnp.int32), doc_ids.astype(jnp.int32)], axis=0)

    def one_block(totals, block_no):
        first_row = (block_no * row_count).astype(jnp.int32)
        query_rows = lax.dynamic_slice_in_dim(queries, first_row, row_count, 0)
        grad_rows = lax.dynamic_slice_in_dim(grad_out, first_row, row_count, 0)
        window = lax.dynamic_slice_in_dim(padded_kv, first_row, key_span, 0)
        key_doc = lax.dynamic_slice_in_dim(padded_doc, first_row, key_span, 0)
        query_doc = lax.dynamic_slice_in_dim(doc_ids.astype(jnp.int32), first_row, row_count, 0)
        query_pos = first_row + jnp.arange(row_count, dtype=jnp.int32)
        key_pos = first_row - REACH * row_count + jnp.arange(key_span, dtype=jnp.int32)
        attended, grad_query, grad_pair = block_grads(query_rows, grad_rows, window, query_pos, key_pos, query_doc, key_doc)
        current = lax.dynamic_slice_in_dim(totals, first_row, key_span, 0)
        totals = lax.dynamic_update_slice_in_dim(totals, current + grad_pair, first_row, 0)
        return totals, (attended, grad_query)

    start_totals = jnp.zeros((REACH * row_count + TOKENS, 2 * HD), jnp.float32)
    totals, (attended, grad_query) = lax.scan(one_block, start_totals, jnp.arange(N_CTX, dtype=jnp.int32))
    grad_pair = totals[REACH * row_count:]
    return (attended.reshape(TOKENS, QH * HD), grad_query.reshape(TOKENS, QH * HD),
            grad_pair[:, :HD].astype(jnp.bfloat16), grad_pair[:, HD:].astype(jnp.bfloat16))
```

```python
import functools

import jax
import jax.numpy as jnp
from jax import lax
from jax.experimental import pallas as pl
from jax.experimental.pallas import tpu as pltpu
from jax.sharding import PartitionSpec as P

LANES = 128
LOG2_E = 1.4426950408889634
MASKED = -1e30

OWN, MATE, LINE, SIDE = range(4)


def nt(a, b):
    return lax.dot_general(a, b, (((1,), (1,)), ((), ())), preferred_element_type=jnp.float32)


def nn(a, b):
    return lax.dot_general(a, b, (((1,), (0,)), ((), ())), preferred_element_type=jnp.float32)


def row_sums(rows):
    high = rows.astype(jnp.bfloat16)
    low = (rows - high.astype(jnp.float32)).astype(jnp.bfloat16)
    ones = jnp.ones((8, rows.shape[1]), jnp.bfloat16)
    return (nt(ones, high) + nt(ones, low))[:1]


def attend_kernel(
    doc_ref, q_ref, g_ref, own_ref, mate_ref, line_ref, side_ref,
    att_ref, gq_ref, own_out, mate_out, line_out, side_out,
    bias, s_ref, e_ref, acc_k, acc_v, kt_ref, vt_ref,
):
    rows, dim = q_ref.shape[0], own_ref.shape[1] // 2
    heads = q_ref.shape[1] // dim
    steps = rows // LANES
    scale = dim**-0.5
    here = lax.axis_index("ctx")
    odd = lax.rem(here, 2)
    count = lax.axis_size("ctx")
    kv_refs = (own_ref, mate_ref, line_ref, side_ref)
    behind = (0, 1 + 2 * odd, 2, 3 - 2 * odd)

    own_doc = jnp.concatenate([doc_ref[pl.ds(here * steps + i, 1), :] for i in range(steps)], axis=1)
    for b in range(4):
        block = here - behind[b]
        valid = block >= 0
        at = lax.rem(block + count, count) * steps
        for i in range(steps):
            row = jnp.where(valid, doc_ref[pl.ds(at + i, 1), :], -1)
            column = jnp.transpose(jnp.broadcast_to(row, (LANES, LANES)).astype(jnp.float32)).astype(jnp.int32)
            same = jnp.concatenate([column] * steps, axis=1) == own_doc
            if b == OWN:
                key_at = lax.broadcasted_iota(jnp.int32, (LANES, rows), 0) + i * LANES
                same = same & (key_at <= lax.broadcasted_iota(jnp.int32, (LANES, rows), 1))
            bias[b, i * LANES : (i + 1) * LANES, :] = jnp.where(same, 0.0, MASKED)
        kt_ref[b] = jnp.transpose(kv_refs[b][:, :dim])
        vt_ref[b] = jnp.transpose(kv_refs[b][:, dim:])

    for h in range(heads):
        cols = slice(h * dim, (h + 1) * dim)
        q, g = q_ref[:, cols], g_ref[:, cols]
        top = None
        for b in range(4):
            s = nt(kv_refs[b][:, :dim], q) + bias[b]
            s_ref[b] = s
            most = jnp.max(s, axis=0, keepdims=True)
            top = most if top is None else jnp.maximum(top, most)
        total, out = 0.0, 0.0
        for b in range(4):
            e = jnp.exp2((s_ref[b] - top) * (scale * LOG2_E))
            e_ref[b] = e
            total = total + jnp.sum(e, axis=0, keepdims=True)
            out = out + nn(vt_ref[b], e.astype(jnp.bfloat16))
        inverse = 1.0 / total
        out = jnp.transpose(out * inverse)
        att_ref[:, cols] = out.astype(jnp.bfloat16)
        delta = row_sums(out * g.astype(jnp.float32))
        grad = 0.0
        for b in range(4):
            probs = e_ref[b] * inverse
            ds = (probs * (nt(kv_refs[b][:, dim:], g) - delta)).astype(jnp.bfloat16)
            gv = nn(probs.astype(jnp.bfloat16), g)
            gk = nn(ds, q)
            acc_v[b] = gv if h == 0 else acc_v[b] + gv
            acc_k[b] = gk if h == 0 else acc_k[b] + gk
            grad = grad + nn(kt_ref[b], ds)
        gq_ref[:, cols] = jnp.transpose(grad * scale).astype(jnp.bfloat16)
    for b, out_ref in enumerate((own_out, mate_out, line_out, side_out)):
        out_ref[:, :dim] = (acc_k[b] * scale).astype(out_ref.dtype)
        out_ref[:, dim:] = acc_v[b].astype(out_ref.dtype)


def attend(docs, queries, grads, own, mate, line, side):
    rows, width = own.shape
    dim = width // 2
    pair = lambda kind: jax.ShapeDtypeStruct((rows, width), kind)
    vmem = pl.BlockSpec(memory_space=pltpu.VMEM)
    return pl.pallas_call(
        attend_kernel,
        out_shape=(
            jax.ShapeDtypeStruct(queries.shape, jnp.bfloat16),
            jax.ShapeDtypeStruct(queries.shape, jnp.bfloat16),
            pair(jnp.float32), pair(jnp.bfloat16), pair(jnp.float32), pair(jnp.bfloat16),
        ),
        in_specs=[vmem] * 7,
        out_specs=[vmem] * 6,
        scratch_shapes=[
            pltpu.VMEM((4, rows, rows), jnp.float32),
            pltpu.VMEM((4, rows, rows), jnp.float32),
            pltpu.VMEM((4, rows, rows), jnp.float32),
            pltpu.VMEM((4, rows, dim), jnp.float32),
            pltpu.VMEM((4, rows, dim), jnp.float32),
            pltpu.VMEM((4, dim, rows), jnp.bfloat16),
            pltpu.VMEM((4, dim, rows), jnp.bfloat16),
        ],
        compiler_params=pltpu.CompilerParams(vmem_limit_bytes=48 << 20),
    )(docs, queries, grads, own, mate, line, side)


def body(queries, key_vectors, value_vectors, doc_ids, grad_out):
    dim = key_vectors.shape[1]
    count = lax.axis_size("ctx")
    to_mate = [(i, i ^ 1) for i in range(count)]
    to_line = [(i, (i + 2) % count) for i in range(count)]
    to_side = [(i, (i + 1 + 2 * (i % 2)) % count) for i in range(count)]
    flip = lambda pairs: [(b, a) for a, b in pairs]

    own = jnp.concatenate([key_vectors, value_vectors], axis=1)
    line = lax.ppermute(own, "ctx", to_line)
    side = lax.ppermute(own, "ctx", to_side)
    mate = lax.ppermute(line, "ctx", to_mate)
    docs = doc_ids.reshape(-1, LANES)
    attended, grad_query, own_part, mate_part, line_part, side_part = attend(
        docs, queries, grad_out, own, mate, line, side
    )
    side_back = lax.ppermute(side_part, "ctx", flip(to_side))
    mate_back = lax.ppermute(mate_part, "ctx", to_mate)
    line_part = (line_part + mate_back.astype(jnp.float32)).astype(jnp.bfloat16)
    line_back = lax.ppermute(line_part, "ctx", flip(to_line))
    total = own_part + side_back.astype(jnp.float32) + line_back.astype(jnp.float32)
    total = total.astype(jnp.bfloat16)
    return attended, grad_query, total[:, :dim], total[:, dim:]


def solution(mesh):
    return jax.shard_map(
        body,
        mesh=mesh,
        in_specs=(P("ctx", "head"), P("ctx", "head"), P("ctx", "head"), P(), P("ctx", "head")),
        out_specs=(P("ctx", "head"), P("ctx", "head"), P("ctx", "head"), P("ctx", "head")),
        check_vma=False,
    )
```

```python
import jax
import jax.numpy as jnp
from jax import lax
from jax.experimental import pallas as pl
from jax.experimental.pallas import tpu as pltpu
from jax.sharding import PartitionSpec as P

LANES = 128
LOG2_E = 1.4426950408889634
MASKED = -1e30

OWN, MATE, LINE, SIDE = range(4)


def nt(a, b):
    return lax.dot_general(a, b, (((1,), (1,)), ((), ())), preferred_element_type=jnp.float32)


def nn(a, b):
    return lax.dot_general(a, b, (((1,), (0,)), ((), ())), preferred_element_type=jnp.float32)


def row_sums(rows):
    high = rows.astype(jnp.bfloat16)
    low = (rows - high.astype(jnp.float32)).astype(jnp.bfloat16)
    ones = jnp.ones((8, rows.shape[1]), jnp.bfloat16)
    return (nt(ones, high) + nt(ones, low))[:1]


def mask_bias(role, doc_ref, bias):
    rows = bias.shape[0]
    steps = rows // LANES
    here, count = lax.axis_index("ctx"), lax.axis_size("ctx")
    odd = lax.rem(here, 2)
    block = here - (0, 1 + 2 * odd, 2, 3 - 2 * odd)[role]
    at = lax.rem(block + count, count) * steps
    own_doc = jnp.concatenate([doc_ref[pl.ds(here * steps + i, 1), :] for i in range(steps)], axis=1)
    for i in range(steps):
        row = jnp.where(block >= 0, doc_ref[pl.ds(at + i, 1), :], -1)
        column = jnp.transpose(jnp.broadcast_to(row, (LANES, LANES)).astype(jnp.float32)).astype(jnp.int32)
        same = jnp.concatenate([column] * steps, axis=1) == own_doc
        if role == OWN:
            key_at = lax.broadcasted_iota(jnp.int32, (LANES, rows), 0) + i * LANES
            same = same & (key_at <= lax.broadcasted_iota(jnp.int32, (LANES, rows), 1))
        bias[i * LANES : (i + 1) * LANES, :] = jnp.where(same, 0.0, MASKED)


def forward(role, doc_ref, q_ref, kv_ref, e_ref, stat_ref, out_ref, bias, s_ref, vt_ref, ready=lambda h: None):
    dim = kv_ref.shape[1] // 2
    heads = q_ref.shape[1] // dim
    factor = dim**-0.5 * LOG2_E
    mask_bias(role, doc_ref, bias)
    vt_ref[...] = jnp.transpose(kv_ref[:, dim:])
    for h in range(heads):
        ready(h)
        s = nt(kv_ref[:, :dim], q_ref[:, h * dim : (h + 1) * dim]) + bias[...]
        s_ref[h] = s
        stat_ref[h : h + 1, :] = jnp.max(s, axis=0, keepdims=True)
    for h in range(heads):
        e = jnp.exp2((s_ref[h] - stat_ref[h : h + 1, :]) * factor)
        e_ref[h] = e.astype(jnp.bfloat16)
        stat_ref[heads + h : heads + h + 1, :] = jnp.sum(e, axis=0, keepdims=True)
    for h in range(heads):
        out_ref[h] = nn(vt_ref[...], e_ref[h])


def backward(q_ref, g_ref, kv_ref, e_ref, scale_ref, delta_ref, part_ref, gq_in, gq_out, kt_ref, p_ref, ds_ref):
    dim = kv_ref.shape[1] // 2
    heads = q_ref.shape[1] // dim
    cols = [slice(h * dim, (h + 1) * dim) for h in range(heads)]
    kt_ref[...] = jnp.transpose(kv_ref[:, :dim])
    for h in range(heads):
        probs = e_ref[h].astype(jnp.float32) * scale_ref[h : h + 1, :]
        p_ref[h] = probs.astype(jnp.bfloat16)
        ds_ref[h] = (probs * (nt(kv_ref[:, dim:], g_ref[:, cols[h]]) - delta_ref[h : h + 1, :])).astype(jnp.bfloat16)
    grad_v = sum(nn(p_ref[h], g_ref[:, cols[h]]) for h in range(heads))
    part_ref[:, dim:] = grad_v.astype(part_ref.dtype)
    grad_k = sum(nn(ds_ref[h], q_ref[:, cols[h]]) for h in range(heads))
    part_ref[:, :dim] = (grad_k * dim**-0.5).astype(part_ref.dtype)
    for h in range(heads):
        grad_q = nn(kt_ref[...], ds_ref[h])
        gq_out(h, grad_q if gq_in is None else gq_in[h] + grad_q)


def store_into(ref):
    def put(h, value):
        ref[h] = value

    return put


def pack_kernel(k_ref, v_ref, kv_ref, sems):
    dim = k_ref.shape[1]
    copies = [
        pltpu.make_async_copy(ref, kv_ref.at[:, i * dim : (i + 1) * dim], sems.at[i]) for i, ref in enumerate((k_ref, v_ref))
    ]
    for copy in copies:
        copy.start()
    for copy in copies:
        copy.wait()


def own_kernel(doc_ref, q_in, g_in, kv_ref, q_ref, g_ref, e_ref, stat_ref, out_ref, bias, s_ref, vt_ref, sems):
    dim = kv_ref.shape[1] // 2
    heads = q_in.shape[1] // dim
    cols = [slice(h * dim, (h + 1) * dim) for h in range(heads)]
    q_copies = [pltpu.make_async_copy(q_in.at[:, c], q_ref.at[:, c], sems.at[0, h]) for h, c in enumerate(cols)]
    g_copies = [pltpu.make_async_copy(g_in.at[:, c], g_ref.at[:, c], sems.at[1, h]) for h, c in enumerate(cols)]
    for copy in q_copies + g_copies:
        copy.start()
    forward(OWN, doc_ref, q_ref, kv_ref, e_ref, stat_ref, out_ref, bias, s_ref, vt_ref, lambda h: q_copies[h].wait())
    for copy in g_copies:
        copy.wait()


def rest_kernel(
    doc_ref, q_ref, g_ref, mate_ref, own_stat, own_o, line_stat, line_o, side_stat, side_o,
    att_ref, mate_part, gq_part, scale_ref, delta_ref,
    bias, s_ref, vt_ref, mate_e, mate_stat, mate_o, kt_ref, p_ref, ds_ref, att_buf, sems,
):
    dim = mate_ref.shape[1] // 2
    heads = q_ref.shape[1] // dim
    factor = dim**-0.5 * LOG2_E
    forward(MATE, doc_ref, q_ref, mate_ref, mate_e, mate_stat, mate_o, bias, s_ref, vt_ref)
    stats = (own_stat, mate_stat, line_stat, side_stat)
    tops = [ref[:heads, :] for ref in stats]
    top = jnp.maximum(jnp.maximum(tops[0], tops[1]), jnp.maximum(tops[2], tops[3]))
    parts = [jnp.exp2((t - top) * factor) for t in tops]
    inverse = 1.0 / sum(p * ref[heads:, :] for p, ref in zip(parts, stats))
    for b in range(4):
        scale_ref[b] = parts[b] * inverse
    copies = []
    for h in range(heads):
        cols = slice(h * dim, (h + 1) * dim)
        out = sum(ref[h] * scale_ref[b, h : h + 1, :] for b, ref in enumerate((own_o, mate_o, line_o, side_o)))
        out = jnp.transpose(out)
        att_buf[:, cols] = out.astype(jnp.bfloat16)
        copies.append(pltpu.make_async_copy(att_buf.at[:, cols], att_ref.at[:, cols], sems.at[h]))
        copies[h].start()
        delta_ref[h : h + 1, :] = row_sums(out * g_ref[:, cols].astype(jnp.float32))
    backward(
        q_ref, g_ref, mate_ref, mate_e, scale_ref.at[MATE], delta_ref, mate_part, None, store_into(gq_part), kt_ref, p_ref, ds_ref
    )
    for copy in copies:
        copy.wait()


def later_kernel(role, q_ref, g_ref, kv_ref, e_ref, scale_ref, delta_ref, gq_in, part_ref, gq_ref, kt_ref, p_ref, ds_ref):
    backward(
        q_ref, g_ref, kv_ref, e_ref, scale_ref.at[role], delta_ref, part_ref, gq_in, store_into(gq_ref), kt_ref, p_ref, ds_ref
    )


def last_kernel(
    role, q_ref, g_ref, kv_ref, e_ref, scale_ref, delta_ref, gq_in, part_ref, gq_ref, kt_ref, p_ref, ds_ref, buf, sems
):
    dim = kv_ref.shape[1] // 2
    copies = []

    def put(h, value):
        cols = slice(h * dim, (h + 1) * dim)
        buf[:, cols] = jnp.transpose(value * dim**-0.5).astype(jnp.bfloat16)
        copies.append(pltpu.make_async_copy(buf.at[:, cols], gq_ref.at[:, cols], sems.at[h]))
        copies[h].start()

    backward(q_ref, g_ref, kv_ref, e_ref, scale_ref.at[role], delta_ref, part_ref, gq_in, put, kt_ref, p_ref, ds_ref)
    for copy in copies:
        copy.wait()


def call(name, kernel, args, outs, scratch, flops, far_in=(), far_out=()):
    near, far = pl.BlockSpec(memory_space=pltpu.VMEM), pl.BlockSpec(memory_space=pltpu.HBM)
    args = [pltpu.with_memory_space_constraint(a, pltpu.HBM) if i in far_in else a for i, a in enumerate(args)]
    return pl.pallas_call(
        kernel,
        name=name,
        out_shape=outs,
        in_specs=[far if i in far_in else near for i in range(len(args))],
        out_specs=[far if i in far_out else near for i in range(len(outs))],
        scratch_shapes=scratch,
        cost_estimate=pl.CostEstimate(flops=flops, bytes_accessed=1 << 20, transcendentals=0),
        compiler_params=pltpu.CompilerParams(vmem_limit_bytes=16 << 20),
    )(*args)


def body(queries, key_vectors, value_vectors, doc_ids, grad_out):
    rows, dim = key_vectors.shape
    heads = queries.shape[1] // dim
    count = lax.axis_size("ctx")
    to_mate = [(i, i ^ 1) for i in range(count)]
    to_line = [(i, (i + 2) % count) for i in range(count)]
    to_side = [(i, (i + 1 + 2 * (i % 2)) % count) for i in range(count)]
    flip = lambda pairs: [(b, a) for a, b in pairs]
    f32, bf16 = jnp.float32, jnp.bfloat16
    shape = jax.ShapeDtypeStruct
    e_shape, stat_shape, out_shape = shape((heads, rows, rows), bf16), shape((2 * heads, rows), f32), shape((heads, dim, rows), f32)
    pair, pair_sent = shape((rows, 2 * dim), f32), shape((rows, 2 * dim), bf16)
    wide = shape(queries.shape, bf16)
    buffer = lambda like: pltpu.VMEM(like.shape, like.dtype)
    flat = pltpu.VMEM((dim, rows), bf16)
    ahead = [pltpu.VMEM((rows, rows), f32), pltpu.VMEM((heads, rows, rows), f32), flat]
    back = [flat, buffer(e_shape), buffer(e_shape)]
    work = 16 * heads * rows * rows * dim

    docs = doc_ids.reshape(-1, LANES)
    own = call(
        "pack", pack_kernel, (key_vectors, value_vectors), (pair_sent,), [pltpu.SemaphoreType.DMA((2,))], 0, (0, 1)
    )[0]
    line = lax.ppermute(own, "ctx", to_line)
    side = lax.ppermute(own, "ctx", to_side)
    q, g, own_e, own_stat, own_o = call(
        "own_forward", own_kernel, (docs, queries, grad_out, own), (wide, wide, e_shape, stat_shape, out_shape),
        [*ahead, pltpu.SemaphoreType.DMA((2, heads))], 2 * work, (1, 2),
    )
    line, own_stat = lax.optimization_barrier((line, own_stat))
    mate = lax.ppermute(line, "ctx", to_mate)

    def first(name, role, kv):
        return call(
            name, lambda *refs: forward(role, *refs), (docs, q, kv), (e_shape, stat_shape, out_shape), ahead, 2 * work
        )

    line_e, line_stat, line_o = first("line_forward", LINE, line)
    side_e, side_stat, side_o = first("side_forward", SIDE, side)
    attended, mate_part, gq, scales, delta = call(
        "rest_forward", rest_kernel,
        (docs, q, g, mate, own_stat, own_o, line_stat, line_o, side_stat, side_o),
        (wide, pair_sent, out_shape, shape((4, heads, rows), f32), shape((heads, rows), f32)),
        [*ahead, buffer(e_shape), buffer(stat_shape), buffer(out_shape), *back, buffer(wide), pltpu.SemaphoreType.DMA((heads,))],
        6 * work, (), (0,),
    )
    mate_back = lax.ppermute(mate_part, "ctx", to_mate)

    def later(name, kernel, role, kv, e, gq, outs, extra=(), far_out=()):
        return call(
            name, lambda *refs: kernel(role, *refs), (q, g, kv, e, scales, delta, gq), outs, [*back, *extra], 4 * work,
            (), far_out,
        )

    line_part, gq = later("line_backward", later_kernel, LINE, line, line_e, gq, (pair, out_shape))
    line_part = (line_part + mate_back.astype(f32)).astype(bf16)
    line_part, gq = lax.optimization_barrier((line_part, gq))
    line_back = lax.ppermute(line_part, "ctx", flip(to_line))
    side_part, gq = later("side_backward", later_kernel, SIDE, side, side_e, gq, (pair_sent, out_shape))
    side_back = lax.ppermute(side_part, "ctx", flip(to_side))
    own_part, grad_query = later(
        "own_backward", last_kernel, OWN, own, own_e, gq, (pair, wide), [buffer(wide), pltpu.SemaphoreType.DMA((heads,))], (1,)
    )
    total = (own_part + side_back.astype(f32) + line_back.astype(f32)).astype(bf16)
    return attended, grad_query, total[:, :dim], total[:, dim:]


def solution(mesh):
    return jax.shard_map(
        body,
        mesh=mesh,
        in_specs=(P("ctx", "head"), P("ctx", "head"), P("ctx", "head"), P(), P("ctx", "head")),
        out_specs=(P("ctx", "head"), P("ctx", "head"), P("ctx", "head"), P("ctx", "head")),
        check_vma=False,
    )
```

```python
import jax
import jax.numpy as jnp
from jax import lax
from jax.experimental import pallas as pl
from jax.experimental.pallas import tpu as pltpu
from jax.sharding import PartitionSpec as P

LANES = 128
LOG2_E = 1.4426950408889634
MASKED = -1e30

OWN, MATE, LINE, SIDE = range(4)


def nt(a, b):
    return lax.dot_general(a, b, (((1,), (1,)), ((), ())), preferred_element_type=jnp.float32)


def nn(a, b):
    return lax.dot_general(a, b, (((1,), (0,)), ((), ())), preferred_element_type=jnp.float32)


def row_sums(rows):
    high = rows.astype(jnp.bfloat16)
    low = (rows - high.astype(jnp.float32)).astype(jnp.bfloat16)
    ones = jnp.ones((8, rows.shape[1]), jnp.bfloat16)
    return (nt(ones, high) + nt(ones, low))[:1]


def mask_bias(role, doc_ref, bias):
    rows = bias.shape[0]
    steps = rows // LANES
    here, count = lax.axis_index("ctx"), lax.axis_size("ctx")
    odd = lax.rem(here, 2)
    block = here - (0, 1 + 2 * odd, 2, 3 - 2 * odd)[role]
    at = lax.rem(block + count, count) * steps
    own_doc = jnp.concatenate([doc_ref[pl.ds(here * steps + i, 1), :] for i in range(steps)], axis=1)
    for i in range(steps):
        row = jnp.where(block >= 0, doc_ref[pl.ds(at + i, 1), :], -1)
        column = jnp.transpose(jnp.broadcast_to(row, (LANES, LANES)).astype(jnp.float32)).astype(jnp.int32)
        same = jnp.concatenate([column] * steps, axis=1) == own_doc
        if role == OWN:
            key_at = lax.broadcasted_iota(jnp.int32, (LANES, rows), 0) + i * LANES
            same = same & (key_at <= lax.broadcasted_iota(jnp.int32, (LANES, rows), 1))
        bias[i * LANES : (i + 1) * LANES, :] = jnp.where(same, 0.0, MASKED)


def forward(role, doc_ref, q_ref, kv_ref, e_ref, stat_ref, out_ref, bias, s_ref, vt_ref, ready=lambda h: None):
    dim = kv_ref.shape[1] // 2
    heads = q_ref.shape[1] // dim
    factor = dim**-0.5 * LOG2_E
    mask_bias(role, doc_ref, bias)
    vt_ref[...] = jnp.transpose(kv_ref[:, dim:])
    for h in range(heads):
        ready(h)
        s = nt(kv_ref[:, :dim], q_ref[:, h * dim : (h + 1) * dim]) + bias[...]
        s_ref[h] = s
        stat_ref[h : h + 1, :] = jnp.max(s, axis=0, keepdims=True)
    for h in range(heads):
        e = jnp.exp2((s_ref[h] - stat_ref[h : h + 1, :]) * factor)
        e_ref[h] = e.astype(jnp.bfloat16)
        stat_ref[heads + h : heads + h + 1, :] = jnp.sum(e, axis=0, keepdims=True)
    for h in range(heads):
        out_ref[h] = nn(vt_ref[...], e_ref[h])


def backward(q_ref, g_ref, kv_ref, e_ref, scale_ref, delta_ref, part_ref, gq_in, gq_out, kt_ref, p_ref, ds_ref):
    dim = kv_ref.shape[1] // 2
    heads = q_ref.shape[1] // dim
    cols = [slice(h * dim, (h + 1) * dim) for h in range(heads)]
    kt_ref[...] = jnp.transpose(kv_ref[:, :dim])
    for h in range(heads):
        probs = e_ref[h].astype(jnp.float32) * scale_ref[h : h + 1, :]
        p_ref[h] = probs.astype(jnp.bfloat16)
        ds_ref[h] = (probs * (nt(kv_ref[:, dim:], g_ref[:, cols[h]]) - delta_ref[h : h + 1, :])).astype(jnp.bfloat16)
    for h in range(heads):
        grad_q = nn(kt_ref[...], ds_ref[h])
        gq_out(h, grad_q if gq_in is None else gq_in[h] + grad_q)
    grad_v = sum(nn(p_ref[h], g_ref[:, cols[h]]) for h in range(heads))
    part_ref[:, dim:] = grad_v.astype(part_ref.dtype)
    grad_k = sum(nn(ds_ref[h], q_ref[:, cols[h]]) for h in range(heads))
    part_ref[:, :dim] = (grad_k * dim**-0.5).astype(part_ref.dtype)


def store_into(ref):
    def put(h, value):
        ref[h] = value

    return put


def pack_kernel(k_ref, v_ref, kv_ref, sems):
    dim = k_ref.shape[1]
    copies = [
        pltpu.make_async_copy(ref, kv_ref.at[:, i * dim : (i + 1) * dim], sems.at[i]) for i, ref in enumerate((k_ref, v_ref))
    ]
    for copy in copies:
        copy.start()
    for copy in copies:
        copy.wait()


def settle_kernel(in_ref, out_ref):
    out_ref[:16, :] = in_ref[:16, :]


def rest_kernel(
    doc_ref, q_ref, g_ref, mate_ref, own_stat, own_o, line_stat, line_o, side_stat, side_o,
    att_ref, mate_part, gq_part, scale_ref, delta_ref,
    bias, s_ref, vt_ref, mate_e, mate_stat, mate_o, kt_ref, p_ref, ds_ref, att_buf, sems,
):
    dim = mate_ref.shape[1] // 2
    heads = q_ref.shape[1] // dim
    factor = dim**-0.5 * LOG2_E
    forward(MATE, doc_ref, q_ref, mate_ref, mate_e, mate_stat, mate_o, bias, s_ref, vt_ref)
    stats = (own_stat, mate_stat, line_stat, side_stat)
    tops = [ref[:heads, :] for ref in stats]
    top = jnp.maximum(jnp.maximum(tops[0], tops[1]), jnp.maximum(tops[2], tops[3]))
    parts = [jnp.exp2((t - top) * factor) for t in tops]
    inverse = 1.0 / sum(p * ref[heads:, :] for p, ref in zip(parts, stats))
    for b in range(4):
        scale_ref[b] = parts[b] * inverse
    copies = []
    for h in range(heads):
        cols = slice(h * dim, (h + 1) * dim)
        out = sum(ref[h] * scale_ref[b, h : h + 1, :] for b, ref in enumerate((own_o, mate_o, line_o, side_o)))
        out = jnp.transpose(out)
        att_buf[:, cols] = out.astype(jnp.bfloat16)
        copies.append(pltpu.make_async_copy(att_buf.at[:, cols], att_ref.at[:, cols], sems.at[h]))
        copies[h].start()
        delta_ref[h : h + 1, :] = row_sums(out * g_ref[:, cols].astype(jnp.float32))
    backward(
        q_ref, g_ref, mate_ref, mate_e, scale_ref.at[MATE], delta_ref, mate_part, None, store_into(gq_part), kt_ref, p_ref, ds_ref
    )
    for copy in copies:
        copy.wait()


def later_kernel(role, q_ref, g_ref, kv_ref, e_ref, scale_ref, delta_ref, gq_in, part_ref, gq_ref, kt_ref, p_ref, ds_ref):
    backward(
        q_ref, g_ref, kv_ref, e_ref, scale_ref.at[role], delta_ref, part_ref, gq_in, store_into(gq_ref), kt_ref, p_ref, ds_ref
    )


def last_kernel(
    role, q_ref, g_ref, kv_ref, e_ref, scale_ref, delta_ref, gq_in, part_ref, gq_ref, kt_ref, p_ref, ds_ref, buf, sems
):
    dim = kv_ref.shape[1] // 2
    copies = []

    def put(h, value):
        cols = slice(h * dim, (h + 1) * dim)
        buf[:, cols] = jnp.transpose(value * dim**-0.5).astype(jnp.bfloat16)
        copies.append(pltpu.make_async_copy(buf.at[:, cols], gq_ref.at[:, cols], sems.at[h]))
        copies[h].start()

    backward(q_ref, g_ref, kv_ref, e_ref, scale_ref.at[role], delta_ref, part_ref, gq_in, put, kt_ref, p_ref, ds_ref)
    for copy in copies:
        copy.wait()


def call(name, kernel, args, outs, scratch, flops, far_in=(), far_out=(), aliases=None):
    near, far = pl.BlockSpec(memory_space=pltpu.VMEM), pl.BlockSpec(memory_space=pltpu.HBM)
    args = [pltpu.with_memory_space_constraint(a, pltpu.HBM) if i in far_in else a for i, a in enumerate(args)]
    return pl.pallas_call(
        kernel,
        name=name,
        out_shape=outs,
        in_specs=[far if i in far_in else near for i in range(len(args))],
        out_specs=[far if i in far_out else near for i in range(len(outs))],
        scratch_shapes=scratch,
        input_output_aliases=aliases or {},
        cost_estimate=pl.CostEstimate(flops=flops, bytes_accessed=0, transcendentals=0),
        compiler_params=pltpu.CompilerParams(vmem_limit_bytes=16 << 20),
    )(*args)


def body(queries, key_vectors, value_vectors, doc_ids, grad_out):
    rows, dim = key_vectors.shape
    heads = queries.shape[1] // dim
    count = lax.axis_size("ctx")
    to_mate = [(i, i ^ 1) for i in range(count)]
    to_line = [(i, (i + 2) % count) for i in range(count)]
    to_side = [(i, (i + 1 + 2 * (i % 2)) % count) for i in range(count)]
    flip = lambda pairs: [(b, a) for a, b in pairs]
    f32, bf16 = jnp.float32, jnp.bfloat16
    shape = jax.ShapeDtypeStruct
    e_shape, stat_shape, out_shape = shape((heads, rows, rows), bf16), shape((2 * heads, rows), f32), shape((heads, dim, rows), f32)
    pair, pair_sent = shape((rows, 2 * dim), f32), shape((rows, 2 * dim), bf16)
    wide = shape(queries.shape, bf16)
    buffer = lambda like: pltpu.VMEM(like.shape, like.dtype)
    flat = pltpu.VMEM((dim, rows), bf16)
    ahead = [pltpu.VMEM((rows, rows), f32), pltpu.VMEM((heads, rows, rows), f32), flat]
    back = [flat, buffer(e_shape), buffer(e_shape)]
    work = heads * rows

    docs = doc_ids.reshape(-1, LANES)
    own = call(
        "pack", pack_kernel, (key_vectors, value_vectors), (pair_sent,), [pltpu.SemaphoreType.DMA((2,))], 0, (0, 1)
    )[0]
    own = call("settle", settle_kernel, (own,), (pair_sent,), [], 1 << 33, (), (), {0: 0})[0]
    line = lax.ppermute(own, "ctx", to_line)
    side = lax.ppermute(own, "ctx", to_side)
    q, g = queries, grad_out

    def first(name, role, kv):
        return call(
            name, lambda *refs: forward(role, *refs), (docs, q, kv), (e_shape, stat_shape, out_shape), ahead, 2 * work
        )

    own_e, own_stat, own_o = first("own_forward", OWN, own)
    line, own_stat = lax.optimization_barrier((line, own_stat))
    mate = lax.ppermute(line, "ctx", to_mate)

    line_e, line_stat, line_o = first("line_forward", LINE, line)
    side_e, side_stat, side_o = first("side_forward", SIDE, side)
    attended, mate_part, gq, scales, delta = call(
        "rest_forward", rest_kernel,
        (docs, q, g, mate, own_stat, own_o, line_stat, line_o, side_stat, side_o),
        (wide, pair_sent, out_shape, shape((4, heads, rows), f32), shape((heads, rows), f32)),
        [*ahead, buffer(e_shape), buffer(stat_shape), buffer(out_shape), *back, buffer(wide), pltpu.SemaphoreType.DMA((heads,))],
        6 * work, (), (0,),
    )
    mate_back = lax.ppermute(mate_part, "ctx", to_mate)

    def later(name, kernel, role, kv, e, gq, outs, extra=(), far_out=()):
        return call(
            name, lambda *refs: kernel(role, *refs), (q, g, kv, e, scales, delta, gq), outs, [*back, *extra], 4 * work,
            (), far_out,
        )

    line_part, gq = later("line_backward", later_kernel, LINE, line, line_e, gq, (pair, out_shape))
    line_part = (line_part + mate_back.astype(f32)).astype(bf16)
    line_part, gq = lax.optimization_barrier((line_part, gq))
    side_part, gq = later("side_backward", later_kernel, SIDE, side, side_e, gq, (pair_sent, out_shape))
    side_back = lax.ppermute(side_part, "ctx", flip(to_side))
    line_back = lax.ppermute(line_part, "ctx", flip(to_line))
    own_part, grad_query = later(
        "own_backward", last_kernel, OWN, own, own_e, gq, (pair, wide), [buffer(wide), pltpu.SemaphoreType.DMA((heads,))], (1,)
    )
    total = lax.optimization_barrier(own_part + line_back.astype(f32))
    total = (total + side_back.astype(f32)).astype(bf16)
    return attended, grad_query, total[:, :dim], total[:, dim:]


def solution(mesh):
    return jax.shard_map(
        body,
        mesh=mesh,
        in_specs=(P("ctx", "head"), P("ctx", "head"), P("ctx", "head"), P(), P("ctx", "head")),
        out_specs=(P("ctx", "head"), P("ctx", "head"), P("ctx", "head"), P("ctx", "head")),
        check_vma=False,
    )
```

```python
import jax
import jax.numpy as jnp
from jax import lax
from jax.experimental import pallas as pl
from jax.experimental.pallas import tpu as pltpu
from jax.sharding import PartitionSpec as P

LANES = 128
LOG2_E = 1.4426950408889634
MASKED = -1e30

OWN, MATE, LINE, SIDE = range(4)


def nt(a, b):
    return lax.dot_general(a, b, (((1,), (1,)), ((), ())), preferred_element_type=jnp.float32)


def nn(a, b):
    return lax.dot_general(a, b, (((1,), (0,)), ((), ())), preferred_element_type=jnp.float32)


def place(role, rows):
    here, count = lax.axis_index("ctx"), lax.axis_size("ctx")
    odd = lax.rem(here, 2)
    block = here - (0, 1 + 2 * odd, 2, 3 - 2 * odd)[role]
    steps = rows // LANES
    return here * steps, lax.rem(block + count, count) * steps, block >= 0


def is_seen(role, doc_ref, rows):
    mine, at, valid = place(role, rows)
    first = jnp.min(doc_ref[pl.ds(mine, 1), :].astype(jnp.float32))
    last = jnp.max(doc_ref[pl.ds(at + rows // LANES - 1, 1), :].astype(jnp.float32))
    return valid & (first == last)


def mask_bias(role, doc_ref, bias):
    rows = bias.shape[0]
    steps = rows // LANES
    mine, at, valid = place(role, rows)
    own_doc = jnp.concatenate([doc_ref[pl.ds(mine + i, 1), :] for i in range(steps)], axis=1)
    for i in range(steps):
        row = jnp.where(valid, doc_ref[pl.ds(at + i, 1), :], -1)
        column = jnp.transpose(jnp.broadcast_to(row, (LANES, LANES)).astype(jnp.float32)).astype(jnp.int32)
        same = jnp.concatenate([column] * steps, axis=1) == own_doc
        if role == OWN:
            key_at = lax.broadcasted_iota(jnp.int32, (LANES, rows), 0) + i * LANES
            same = same & (key_at <= lax.broadcasted_iota(jnp.int32, (LANES, rows), 1))
        bias[i * LANES : (i + 1) * LANES, :] = jnp.where(same, 0.0, MASKED)


def forward(q_ref, kv_ref, bias, e_ref, stat_ref, out_ref, s_ref, vt_ref):
    dim = kv_ref.shape[1] // 2
    heads = q_ref.shape[1] // dim
    factor = dim**-0.5 * LOG2_E
    vt_ref[...] = jnp.transpose(kv_ref[:, dim:])
    for h in range(heads):
        s = nt(kv_ref[:, :dim], q_ref[:, h * dim : (h + 1) * dim]) + bias[...]
        s_ref[h] = s
        stat_ref[h : h + 1, :] = jnp.max(s, axis=0, keepdims=True)
    for h in range(heads):
        e = jnp.exp2((s_ref[h] - stat_ref[h : h + 1, :]) * factor)
        e_ref[h] = e.astype(jnp.bfloat16)
        stat_ref[heads + h : heads + h + 1, :] = jnp.sum(e, axis=0, keepdims=True)
    for h in range(heads):
        out_ref[h] = nn(vt_ref[...], e_ref[h])


def forward_unseen(stat_ref, out_ref):
    heads = out_ref.shape[0]
    stat_ref[:heads, :] = jnp.full((heads, stat_ref.shape[1]), MASKED, jnp.float32)
    stat_ref[heads:, :] = jnp.zeros((heads, stat_ref.shape[1]), jnp.float32)
    out_ref[...] = jnp.zeros(out_ref.shape, out_ref.dtype)


def backward_queries(g_ref, kv_ref, e_ref, scale_ref, delta_ref, gq_out, kt_ref, p_ref, ds_ref, dp=None):
    dim = kv_ref.shape[1] // 2
    heads = g_ref.shape[1] // dim
    kt_ref[...] = jnp.transpose(kv_ref[:, :dim])
    for h in range(heads):
        probs = e_ref[h].astype(jnp.float32) * scale_ref[h : h + 1, :]
        p_ref[h] = probs.astype(jnp.bfloat16)
        grad_p = nt(kv_ref[:, dim:], g_ref[:, h * dim : (h + 1) * dim]) if dp is None else dp[h]
        ds_ref[h] = (probs * (grad_p - delta_ref[h : h + 1, :])).astype(jnp.bfloat16)
    for h in range(heads):
        gq_out(h, nn(kt_ref[...], ds_ref[h]))


def backward_keys(q_ref, g_ref, p_ref, ds_ref, part_ref):
    dim = part_ref.shape[1] // 2
    cols = [slice(h * dim, (h + 1) * dim) for h in range(q_ref.shape[1] // dim)]
    grad_v = sum(nn(p_ref[h], g_ref[:, c]) for h, c in enumerate(cols))
    part_ref[:, dim:] = grad_v.astype(part_ref.dtype)
    grad_k = sum(nn(ds_ref[h], q_ref[:, c]) for h, c in enumerate(cols))
    part_ref[:, :dim] = (grad_k * dim**-0.5).astype(part_ref.dtype)


def backward_unseen(part_ref, gq_in, gq_ref):
    part_ref[...] = jnp.zeros(part_ref.shape, part_ref.dtype)
    gq_ref[...] = jnp.zeros(gq_ref.shape, gq_ref.dtype) if gq_in is None else gq_in[...]


def pack_kernel(k_ref, v_ref, kv_ref, sems):
    dim = k_ref.shape[1]
    copies = [
        pltpu.make_async_copy(ref, kv_ref.at[:, i * dim : (i + 1) * dim], sems.at[i]) for i, ref in enumerate((k_ref, v_ref))
    ]
    for copy in copies:
        copy.start()
    for copy in copies:
        copy.wait()


def settle_kernel(in_ref, out_ref):
    out_ref[:16, :] = in_ref[:16, :]


def own_kernel(doc_ref, q_ref, g_ref, kv_ref, e_ref, stat_ref, out_ref, bias_ref, gt_ref, dp_ref, bias, s_ref, vt_ref):
    dim = kv_ref.shape[1] // 2
    heads = q_ref.shape[1] // dim
    mask_bias(OWN, doc_ref, bias)
    forward(q_ref, kv_ref, bias, e_ref, stat_ref, out_ref, s_ref, vt_ref)
    for role in (MATE, LINE, SIDE):
        mask_bias(role, doc_ref, bias_ref.at[role - 1])
    for h in range(heads):
        g = g_ref[:, h * dim : (h + 1) * dim]
        gt_ref[h] = jnp.transpose(g)
        dp_ref[h] = nt(kv_ref[:, dim:], g)


def next_kernel(role, doc_ref, q_ref, kv_ref, bias_ref, e_ref, stat_ref, out_ref, s_ref, vt_ref):
    seen = is_seen(role, doc_ref, kv_ref.shape[0])

    @pl.when(seen)
    def _():
        forward(q_ref, kv_ref, bias_ref.at[role - 1], e_ref, stat_ref, out_ref, s_ref, vt_ref)

    @pl.when(jnp.logical_not(seen))
    def _():
        forward_unseen(stat_ref, out_ref)


def next_backward(seen, q_ref, g_ref, kv_ref, e_ref, scale_ref, delta_ref, gq_in, part_ref, gq_ref, kt_ref, p_ref, ds_ref):
    @pl.when(seen)
    def _():
        def put(h, value):
            gq_ref[h] = value if gq_in is None else gq_in[h] + value

        backward_queries(g_ref, kv_ref, e_ref, scale_ref, delta_ref, put, kt_ref, p_ref, ds_ref)
        backward_keys(q_ref, g_ref, p_ref, ds_ref, part_ref)

    @pl.when(jnp.logical_not(seen))
    def _():
        backward_unseen(part_ref, gq_in, gq_ref)


def rest_kernel(
    doc_ref, q_ref, g_ref, mate_ref, bias_ref, gt_ref, own_stat, own_o, line_stat, line_o, side_stat, side_o,
    att_t, mate_part, gq_part, scale_ref, delta_ref,
    s_ref, vt_ref, mate_e, mate_stat, mate_o, kt_ref, p_ref, ds_ref,
):
    dim = mate_ref.shape[1] // 2
    heads = q_ref.shape[1] // dim
    factor = dim**-0.5 * LOG2_E
    next_kernel(MATE, doc_ref, q_ref, mate_ref, bias_ref, mate_e, mate_stat, mate_o, s_ref, vt_ref)
    stats = (own_stat, mate_stat, line_stat, side_stat)
    tops = [ref[:heads, :] for ref in stats]
    top = jnp.maximum(jnp.maximum(tops[0], tops[1]), jnp.maximum(tops[2], tops[3]))
    parts = [jnp.exp2((t - top) * factor) for t in tops]
    inverse = 1.0 / sum(p * ref[heads:, :] for p, ref in zip(parts, stats))
    for b in range(4):
        scale_ref[b] = parts[b] * inverse
    for h in range(heads):
        out = sum(ref[h] * scale_ref[b, h : h + 1, :] for b, ref in enumerate((own_o, mate_o, line_o, side_o)))
        att_t[h] = out.astype(jnp.bfloat16)
        delta_ref[h : h + 1, :] = jnp.sum(out * gt_ref[h].astype(jnp.float32), axis=0, keepdims=True)
    next_backward(
        is_seen(MATE, doc_ref, mate_ref.shape[0]), q_ref, g_ref, mate_ref, mate_e, scale_ref.at[MATE], delta_ref, None,
        mate_part, gq_part, kt_ref, p_ref, ds_ref,
    )


def line_kernel(
    doc_ref, q_ref, g_ref, kv_ref, e_ref, side_ref, side_e, scale_ref, delta_ref, gq_in,
    part_ref, side_part, gq_ref, kt_ref, p_ref, ds_ref,
):
    rows = kv_ref.shape[0]
    first_chip = lax.axis_index("ctx") < 2
    common = (q_ref, g_ref)

    @pl.when(jnp.logical_not(first_chip))
    def _():
        next_backward(
            is_seen(LINE, doc_ref, rows), *common, kv_ref, e_ref, scale_ref.at[LINE], delta_ref, gq_in,
            part_ref, gq_ref, kt_ref, p_ref, ds_ref,
        )

    @pl.when(first_chip)
    def _():
        part_ref[...] = jnp.zeros(part_ref.shape, part_ref.dtype)
        next_backward(
            is_seen(SIDE, doc_ref, rows), *common, side_ref, side_e, scale_ref.at[SIDE], delta_ref, gq_in,
            side_part, gq_ref, kt_ref, p_ref, ds_ref,
        )


def turn(h, value, buf):
    buf[:, h * value.shape[0] : (h + 1) * value.shape[0]] = jnp.transpose(value.astype(jnp.bfloat16))


def side_kernel(
    doc_ref, q_ref, g_ref, kv_ref, e_ref, scale_ref, delta_ref, gq_in, early_part, part_ref, gq_ref, kt_ref, p_ref, ds_ref
):
    first_chip = lax.axis_index("ctx") < 2

    @pl.when(jnp.logical_not(first_chip))
    def _():
        next_backward(
            is_seen(SIDE, doc_ref, kv_ref.shape[0]), q_ref, g_ref, kv_ref, e_ref, scale_ref.at[SIDE], delta_ref, gq_in,
            part_ref, gq_ref, kt_ref, p_ref, ds_ref,
        )

    @pl.when(first_chip)
    def _():
        part_ref[...] = early_part[...]
        gq_ref[...] = gq_in[...]


def last_kernel(
    q_ref, g_ref, kv_ref, e_ref, scale_ref, delta_ref, gq_in, dp_ref, att_t, part_ref, gq_ref, att_ref,
    kt_ref, p_ref, ds_ref, buf, att_buf, sems,
):
    factor = (kv_ref.shape[1] // 2) ** -0.5
    for h in range(att_t.shape[0]):
        turn(h, att_t[h], att_buf)
    att_copy = pltpu.make_async_copy(att_buf, att_ref, sems.at[0])
    gq_copy = pltpu.make_async_copy(buf, gq_ref, sems.at[1])
    att_copy.start()

    @pl.when(lax.axis_index("ctx") >= 0)
    def _():
        backward_queries(
            g_ref, kv_ref, e_ref, scale_ref.at[OWN], delta_ref, lambda h, v: turn(h, (gq_in[h] + v) * factor, buf),
            kt_ref, p_ref, ds_ref, dp_ref,
        )

    gq_copy.start()

    @pl.when(lax.axis_index("ctx") >= 0)
    def _():
        backward_keys(q_ref, g_ref, p_ref, ds_ref, part_ref)

    att_copy.wait()
    gq_copy.wait()


def line_add_kernel(line_ref, mate_ref, out_ref):
    out_ref[...] = (line_ref[...] + mate_ref[...].astype(jnp.float32)).astype(jnp.bfloat16)


def line_sum_kernel(own_ref, line_ref, out_ref):
    out_ref[...] = own_ref[...] + line_ref[...].astype(jnp.float32)


def side_sum_kernel(sum_ref, near_ref, far_ref, k_ref, v_ref):
    here, count = lax.axis_index("ctx"), lax.axis_size("ctx")
    dim = k_ref.shape[1]
    even = lax.rem(here, 2) == 0
    side = jnp.where(even, near_ref[...].astype(jnp.float32), far_ref[...].astype(jnp.float32))
    total = sum_ref[...] + jnp.where(even | (here + 3 < count), side, 0.0)
    k_ref[...] = total[:, :dim].astype(jnp.bfloat16)
    v_ref[...] = total[:, dim:].astype(jnp.bfloat16)


def call(name, kernel, args, outs, scratch, flops, far_in=(), far_out=(), aliases=None):
    near, far = pl.BlockSpec(memory_space=pltpu.VMEM), pl.BlockSpec(memory_space=pltpu.HBM)
    args = [pltpu.with_memory_space_constraint(a, pltpu.HBM) if i in far_in else a for i, a in enumerate(args)]
    return pl.pallas_call(
        kernel,
        name=name,
        out_shape=outs,
        in_specs=[far if i in far_in else near for i in range(len(args))],
        out_specs=[far if i in far_out else near for i in range(len(outs))],
        scratch_shapes=scratch,
        input_output_aliases=aliases or {},
        cost_estimate=pl.CostEstimate(flops=flops, bytes_accessed=0, transcendentals=0),
        compiler_params=pltpu.CompilerParams(vmem_limit_bytes=16 << 20),
    )(*args)


def three_back(count):
    to = {i: i - 3 for i in range(4, count, 2)}
    to.update({i: i + 3 for i in range(3, count - 3, 2)})
    to.update({0: 2, 1: 0, 2: 4, count - 3: count - 1, count - 1: count - 3})
    return list(to.items())


def body(queries, key_vectors, value_vectors, doc_ids, grad_out):
    rows, dim = key_vectors.shape
    heads = queries.shape[1] // dim
    count = lax.axis_size("ctx")
    to_mate = [(i, i ^ 1) for i in range(count)]
    to_line = [(i, (i + 2) % count) for i in range(count)]
    to_side = [(i, (i + 1 + 2 * (i % 2)) % count) for i in range(count)]
    flip = lambda pairs: [(b, a) for a, b in pairs]
    f32, bf16 = jnp.float32, jnp.bfloat16
    shape = jax.ShapeDtypeStruct
    e_shape, stat_shape, out_shape = shape((heads, rows, rows), bf16), shape((2 * heads, rows), f32), shape((heads, dim, rows), f32)
    pair, pair_sent = shape((rows, 2 * dim), f32), shape((rows, 2 * dim), bf16)
    wide = shape(queries.shape, bf16)
    buffer = lambda like: pltpu.VMEM(like.shape, like.dtype)
    flat = pltpu.VMEM((dim, rows), bf16)
    ahead = [pltpu.VMEM((heads, rows, rows), f32), flat]
    back = [flat, buffer(e_shape), buffer(e_shape)]
    work = heads * rows

    docs = doc_ids.reshape(-1, LANES)
    own = call(
        "pack", pack_kernel, (key_vectors, value_vectors), (pair_sent,), [pltpu.SemaphoreType.DMA((2,))], 0, (0, 1)
    )[0]
    own = call("settle", settle_kernel, (own,), (pair_sent,), [], 1 << 33, (), (), {0: 0})[0]
    line = lax.ppermute(own, "ctx", to_line)
    q, g = queries, grad_out
    own_e, own_stat, own_o, bias, gt, dp = call(
        "own_forward", own_kernel, (docs, q, g, own),
        (e_shape, stat_shape, out_shape, shape((3, rows, rows), f32), shape((heads, dim, rows), bf16), shape((heads, rows, rows), f32)),
        [pltpu.VMEM((rows, rows), f32), *ahead], work,
    )
    line, own_stat = lax.optimization_barrier((line, own_stat))
    side = lax.ppermute(own, "ctx", to_side)
    mate = lax.ppermute(line, "ctx", to_mate)

    def first(name, role, kv):
        return call(
            name, lambda *refs: next_kernel(role, *refs), (docs, q, kv, bias), (e_shape, stat_shape, out_shape), ahead, work
        )

    line_e, line_stat, line_o = first("line_forward", LINE, line)
    side_e, side_stat, side_o = first("side_forward", SIDE, side)
    attended_t, mate_part, gq, scales, delta = call(
        "rest_forward", rest_kernel,
        (docs, q, g, mate, bias, gt, own_stat, own_o, line_stat, line_o, side_stat, side_o),
        (shape((heads, dim, rows), bf16), pair_sent, out_shape, shape((4, heads, rows), f32), shape((heads, rows), f32)),
        [*ahead, buffer(e_shape), buffer(stat_shape), buffer(out_shape), *back],
        work,
    )
    mate_back = lax.ppermute(mate_part, "ctx", to_mate)
    line_part, early_part, gq = call(
        "line_backward", line_kernel, (docs, q, g, line, line_e, side, side_e, scales, delta, gq), (pair, pair_sent, out_shape),
        back, work,
    )
    line_part = call("line_add", line_add_kernel, (line_part, mate_back), (pair_sent,), [], 0)[0]
    line_part, gq = lax.optimization_barrier((line_part, gq))
    side_part, gq = call(
        "side_backward", side_kernel, (docs, q, g, side, side_e, scales, delta, gq, early_part), (pair_sent, out_shape), back, work
    )
    side_far = lax.ppermute(side_part, "ctx", three_back(count))
    side_near = lax.ppermute(side_part, "ctx", to_mate)
    line_back = lax.ppermute(line_part, "ctx", flip(to_line))
    own_part, grad_query, attended = call(
        "own_backward", last_kernel, (q, g, own, own_e, scales, delta, gq, dp, attended_t), (pair, wide, wide),
        [*back, buffer(wide), buffer(wide), pltpu.SemaphoreType.DMA((2,))], work, (), (1, 2),
    )
    total = call("line_sum", line_sum_kernel, (own_part, line_back), (pair,), [], work)[0]
    narrow = shape((rows, dim), bf16)
    grad_key, grad_value = call("side_sum", side_sum_kernel, (total, side_near, side_far), (narrow, narrow), [], 0)
    return attended, grad_query, grad_key, grad_value


def solution(mesh):
    return jax.shard_map(
        body,
        mesh=mesh,
        in_specs=(P("ctx", "head"), P("ctx", "head"), P("ctx", "head"), P(), P("ctx", "head")),
        out_specs=(P("ctx", "head"), P("ctx", "head"), P("ctx", "head"), P("ctx", "head")),
        check_vma=False,
    )
```

```python
import jax
import jax.numpy as jnp
from jax import lax
from jax.experimental import pallas as pl
from jax.experimental.pallas import tpu as pltpu
from jax.sharding import PartitionSpec as P

LANES = 128
LOG2_E = 1.4426950408889634
MASKED = -1e30

OWN, MATE, LINE, SIDE = range(4)


def nt(a, b):
    return lax.dot_general(a, b, (((1,), (1,)), ((), ())), preferred_element_type=jnp.float32)


def nn(a, b):
    return lax.dot_general(a, b, (((1,), (0,)), ((), ())), preferred_element_type=jnp.float32)


def place(role, rows):
    here, count = lax.axis_index("ctx"), lax.axis_size("ctx")
    odd = lax.rem(here, 2)
    block = here - (0, 1 + 2 * odd, 2, 3 - 2 * odd)[role]
    steps = rows // LANES
    return here * steps, lax.rem(block + count, count) * steps, block >= 0


def is_seen(role, doc_ref, rows):
    mine, at, valid = place(role, rows)
    first = jnp.min(doc_ref[pl.ds(mine, 1), :].astype(jnp.float32))
    last = jnp.max(doc_ref[pl.ds(at + rows // LANES - 1, 1), :].astype(jnp.float32))
    return valid & (first == last)


def mask_bias(role, doc_ref, bias):
    rows = bias.shape[0]
    steps = rows // LANES
    mine, at, valid = place(role, rows)
    own_doc = jnp.concatenate([doc_ref[pl.ds(mine + i, 1), :] for i in range(steps)], axis=1)
    for i in range(steps):
        row = jnp.where(valid, doc_ref[pl.ds(at + i, 1), :], -1)
        column = jnp.transpose(jnp.broadcast_to(row, (LANES, LANES)).astype(jnp.float32)).astype(jnp.int32)
        same = jnp.concatenate([column] * steps, axis=1) == own_doc
        if role == OWN:
            key_at = lax.broadcasted_iota(jnp.int32, (LANES, rows), 0) + i * LANES
            same = same & (key_at <= lax.broadcasted_iota(jnp.int32, (LANES, rows), 1))
        bias[i * LANES : (i + 1) * LANES, :] = jnp.where(same, 0.0, MASKED)


def forward(q_ref, kv_ref, bias, gt_ref, e_ref, stat_ref, out_ref, s_ref, vt_ref):
    dim = kv_ref.shape[1] // 2
    heads = q_ref.shape[1] // dim
    factor = dim**-0.5 * LOG2_E
    vt_ref[...] = jnp.transpose(kv_ref[:, dim:])
    for h in range(heads):
        s_ref[h] = nt(kv_ref[:, :dim], q_ref[:, h * dim : (h + 1) * dim])
    for h in range(heads):
        s = s_ref[h] * factor + bias[...]
        top = jnp.max(s, axis=0, keepdims=True)
        e = jnp.exp2(s - top)
        e_ref[h] = e.astype(jnp.bfloat16)
        stat_ref[h : h + 1, :] = top
        stat_ref[heads + h : heads + h + 1, :] = jnp.sum(e, axis=0, keepdims=True)
    for h in range(heads):
        out = nn(vt_ref[...], e_ref[h])
        out_ref[h] = out
        stat_ref[2 * heads + h : 2 * heads + h + 1, :] = jnp.sum(out * gt_ref[h].astype(jnp.float32), axis=0, keepdims=True)


def forward_unseen(stat_ref, out_ref):
    heads = out_ref.shape[0]
    stat_ref[:heads, :] = jnp.full((heads, stat_ref.shape[1]), MASKED, jnp.float32)
    stat_ref[heads:, :] = jnp.zeros((2 * heads, stat_ref.shape[1]), jnp.float32)
    out_ref[...] = jnp.zeros(out_ref.shape, out_ref.dtype)


def backward_queries(g_ref, kv_ref, e_ref, scale_ref, delta_ref, gq_out, kt_ref, p_ref, ds_ref, dp=None):
    dim = kv_ref.shape[1] // 2
    heads = g_ref.shape[1] // dim
    kt_ref[...] = jnp.transpose(kv_ref[:, :dim])
    for h in range(heads):
        probs = e_ref[h] * scale_ref[h : h + 1, :].astype(jnp.bfloat16)
        p_ref[h] = probs
        grad_p = nt(kv_ref[:, dim:], g_ref[:, h * dim : (h + 1) * dim]) if dp is None else dp[h]
        ds_ref[h] = probs * (grad_p - delta_ref[h : h + 1, :]).astype(jnp.bfloat16)
    for h in range(heads):
        gq_out(h, nn(kt_ref[...], ds_ref[h]))


def backward_keys(q_ref, g_ref, p_ref, ds_ref, part_ref):
    dim = part_ref.shape[1] // 2
    cols = [slice(h * dim, (h + 1) * dim) for h in range(q_ref.shape[1] // dim)]
    grad_v = sum(nn(p_ref[h], g_ref[:, c]) for h, c in enumerate(cols))
    part_ref[:, dim:] = grad_v.astype(part_ref.dtype)
    grad_k = sum(nn(ds_ref[h], q_ref[:, c]) for h, c in enumerate(cols))
    part_ref[:, :dim] = (grad_k * dim**-0.5).astype(part_ref.dtype)


def backward_unseen(part_ref, gq_in, gq_ref):
    part_ref[...] = jnp.zeros(part_ref.shape, part_ref.dtype)
    gq_ref[...] = jnp.zeros(gq_ref.shape, gq_ref.dtype) if gq_in is None else gq_in[...]


def pack_kernel(k_ref, v_ref, kv_ref, sems):
    dim = k_ref.shape[1]
    copies = [
        pltpu.make_async_copy(ref, kv_ref.at[:, i * dim : (i + 1) * dim], sems.at[i]) for i, ref in enumerate((k_ref, v_ref))
    ]
    for copy in copies:
        copy.start()
    for copy in copies:
        copy.wait()


def settle_kernel(in_ref, out_ref):
    out_ref[:16, :] = in_ref[:16, :]


def own_kernel(doc_ref, q_ref, g_ref, kv_ref, e_ref, stat_ref, out_ref, bias_ref, gt_ref, dp_ref, bias, s_ref, vt_ref):
    dim = kv_ref.shape[1] // 2
    heads = q_ref.shape[1] // dim
    mask_bias(OWN, doc_ref, bias)
    for h in range(heads):
        gt_ref[h] = jnp.transpose(g_ref[:, h * dim : (h + 1) * dim])
    forward(q_ref, kv_ref, bias, gt_ref, e_ref, stat_ref, out_ref, s_ref, vt_ref)
    for role in (MATE, LINE, SIDE):
        mask_bias(role, doc_ref, bias_ref.at[role - 1])
    for h in range(heads):
        dp_ref[h] = nt(kv_ref[:, dim:], g_ref[:, h * dim : (h + 1) * dim])


def next_kernel(role, doc_ref, q_ref, kv_ref, bias_ref, gt_ref, e_ref, stat_ref, out_ref, s_ref, vt_ref):
    seen = is_seen(role, doc_ref, kv_ref.shape[0])

    @pl.when(seen)
    def _():
        forward(q_ref, kv_ref, bias_ref.at[role - 1], gt_ref, e_ref, stat_ref, out_ref, s_ref, vt_ref)

    @pl.when(jnp.logical_not(seen))
    def _():
        forward_unseen(stat_ref, out_ref)


def next_backward(seen, q_ref, g_ref, kv_ref, e_ref, scale_ref, delta_ref, gq_in, part_ref, gq_ref, kt_ref, p_ref, ds_ref):
    def run():
        def put(h, value):
            gq_ref[h] = value if gq_in is None else gq_in[h] + value

        backward_queries(g_ref, kv_ref, e_ref, scale_ref, delta_ref, put, kt_ref, p_ref, ds_ref)
        backward_keys(q_ref, g_ref, p_ref, ds_ref, part_ref)

    if seen is True:
        run()
        return
    pl.when(seen)(run)

    @pl.when(jnp.logical_not(seen))
    def _():
        backward_unseen(part_ref, gq_in, gq_ref)


def rest_kernel(
    doc_ref, q_ref, g_ref, mate_ref, side_ref, bias_ref, gt_ref, own_stat, line_stat, side_stat, side_e,
    mate_o, mate_part, side_part, gq_part, scale_ref, delta_ref,
    s_ref, vt_ref, mate_e, mate_stat, kt_ref, p_ref, ds_ref,
):
    dim = mate_ref.shape[1] // 2
    heads = q_ref.shape[1] // dim
    next_kernel(MATE, doc_ref, q_ref, mate_ref, bias_ref, gt_ref, mate_e, mate_stat, mate_o, s_ref, vt_ref)
    stats = (own_stat, mate_stat, line_stat, side_stat)
    tops = [ref[:heads, :] for ref in stats]
    top = jnp.maximum(jnp.maximum(tops[0], tops[1]), jnp.maximum(tops[2], tops[3]))
    parts = [jnp.exp2(t - top) for t in tops]
    inverse = 1.0 / sum(p * ref[heads : 2 * heads, :] for p, ref in zip(parts, stats))
    for b in range(4):
        scale_ref[b] = parts[b] * inverse
    delta_ref[...] = sum(p * ref[2 * heads :, :] for p, ref in zip(parts, stats)) * inverse
    rows = mate_ref.shape[0]
    seen = is_seen(MATE, doc_ref, rows)

    @pl.when(seen)
    def _():
        next_backward(
            True, q_ref, g_ref, mate_ref, mate_e, scale_ref.at[MATE], delta_ref, None, mate_part, gq_part, kt_ref, p_ref, ds_ref
        )

    @pl.when(jnp.logical_not(seen))
    def _():
        mate_part[...] = jnp.zeros(mate_part.shape, mate_part.dtype)
        next_backward(
            is_seen(SIDE, doc_ref, rows), q_ref, g_ref, side_ref, side_e, scale_ref.at[SIDE], delta_ref, None,
            side_part, gq_part, kt_ref, p_ref, ds_ref,
        )


def line_kernel(doc_ref, q_ref, g_ref, kv_ref, e_ref, scale_ref, delta_ref, gq_in, part_ref, gq_ref, kt_ref, p_ref, ds_ref):
    next_backward(
        is_seen(LINE, doc_ref, kv_ref.shape[0]), q_ref, g_ref, kv_ref, e_ref, scale_ref.at[LINE], delta_ref, gq_in,
        part_ref, gq_ref, kt_ref, p_ref, ds_ref,
    )


def side_kernel(
    doc_ref, q_ref, g_ref, kv_ref, e_ref, scale_ref, delta_ref, gq_in, early_part, part_ref, gq_ref, kt_ref, p_ref, ds_ref
):
    rows = kv_ref.shape[0]
    late = is_seen(MATE, doc_ref, rows)

    @pl.when(late)
    def _():
        next_backward(
            is_seen(SIDE, doc_ref, rows), q_ref, g_ref, kv_ref, e_ref, scale_ref.at[SIDE], delta_ref, gq_in,
            part_ref, gq_ref, kt_ref, p_ref, ds_ref,
        )

    @pl.when(jnp.logical_not(late))
    def _():
        part_ref[...] = early_part[...]
        gq_ref[...] = gq_in[...]


def turn(h, value, buf):
    buf[:, h * value.shape[0] : (h + 1) * value.shape[0]] = jnp.transpose(value.astype(jnp.bfloat16))


def last_kernel(
    q_ref, g_ref, kv_ref, e_ref, scale_ref, delta_ref, gq_in, dp_ref, own_o, mate_o, line_o, side_o, part_ref, gq_ref, att_ref,
    kt_ref, p_ref, ds_ref, buf, att_buf, sems,
):
    factor = (kv_ref.shape[1] // 2) ** -0.5
    for h in range(own_o.shape[0]):
        out = sum(ref[h] * scale_ref[b, h : h + 1, :] for b, ref in enumerate((own_o, mate_o, line_o, side_o)))
        turn(h, out, att_buf)
    att_copy = pltpu.make_async_copy(att_buf, att_ref, sems.at[0])
    gq_copy = pltpu.make_async_copy(buf, gq_ref, sems.at[1])
    att_copy.start()

    @pl.when(lax.axis_index("ctx") >= 0)
    def _():
        backward_queries(
            g_ref, kv_ref, e_ref, scale_ref.at[OWN], delta_ref, lambda h, v: turn(h, (gq_in[h] + v) * factor, buf),
            kt_ref, p_ref, ds_ref, dp_ref,
        )

    gq_copy.start()

    @pl.when(lax.axis_index("ctx") >= 0)
    def _():
        backward_keys(q_ref, g_ref, p_ref, ds_ref, part_ref)

    att_copy.wait()
    gq_copy.wait()


def line_add_kernel(line_ref, mate_ref, out_ref):
    out_ref[...] = (line_ref[...] + mate_ref[...].astype(jnp.float32)).astype(jnp.bfloat16)


def line_sum_kernel(own_ref, line_ref, out_ref):
    out_ref[...] = own_ref[...] + line_ref[...].astype(jnp.float32)


def side_sum_kernel(sum_ref, near_ref, far_ref, k_ref, v_ref):
    here, count = lax.axis_index("ctx"), lax.axis_size("ctx")
    dim = k_ref.shape[1]
    even = lax.rem(here, 2) == 0
    side = jnp.where(even, near_ref[...].astype(jnp.float32), far_ref[...].astype(jnp.float32))
    total = sum_ref[...] + jnp.where(even | (here + 3 < count), side, 0.0)
    k_ref[...] = total[:, :dim].astype(jnp.bfloat16)
    v_ref[...] = total[:, dim:].astype(jnp.bfloat16)


def call(name, kernel, args, outs, scratch, flops, far_in=(), far_out=(), aliases=None):
    near, far = pl.BlockSpec(memory_space=pltpu.VMEM), pl.BlockSpec(memory_space=pltpu.HBM)
    args = [pltpu.with_memory_space_constraint(a, pltpu.HBM) if i in far_in else a for i, a in enumerate(args)]
    return pl.pallas_call(
        kernel,
        name=name,
        out_shape=outs,
        in_specs=[far if i in far_in else near for i in range(len(args))],
        out_specs=[far if i in far_out else near for i in range(len(outs))],
        scratch_shapes=scratch,
        input_output_aliases=aliases or {},
        cost_estimate=pl.CostEstimate(flops=flops, bytes_accessed=0, transcendentals=0),
        compiler_params=pltpu.CompilerParams(vmem_limit_bytes=16 << 20),
    )(*args)


def three_back(count):
    to = {i: i - 3 for i in range(4, count, 2)}
    to.update({i: i + 3 for i in range(3, count - 3, 2)})
    to.update({0: 2, 1: 0, 2: 4, count - 3: count - 1, count - 1: count - 3})
    return list(to.items())


def body(queries, key_vectors, value_vectors, doc_ids, grad_out):
    rows, dim = key_vectors.shape
    heads = queries.shape[1] // dim
    count = lax.axis_size("ctx")
    to_mate = [(i, i ^ 1) for i in range(count)]
    to_line = [(i, (i + 2) % count) for i in range(count)]
    to_side = [(i, (i + 1 + 2 * (i % 2)) % count) for i in range(count)]
    flip = lambda pairs: [(b, a) for a, b in pairs]
    f32, bf16 = jnp.float32, jnp.bfloat16
    shape = jax.ShapeDtypeStruct
    e_shape, stat_shape, out_shape = shape((heads, rows, rows), bf16), shape((3 * heads, rows), f32), shape((heads, dim, rows), f32)
    pair, pair_sent = shape((rows, 2 * dim), f32), shape((rows, 2 * dim), bf16)
    wide = shape(queries.shape, bf16)
    buffer = lambda like: pltpu.VMEM(like.shape, like.dtype)
    flat = pltpu.VMEM((dim, rows), bf16)
    ahead = [pltpu.VMEM((heads, rows, rows), f32), flat]
    back = [flat, buffer(e_shape), buffer(e_shape)]
    work = heads * rows

    docs = doc_ids.reshape(-1, LANES)
    own = call(
        "pack", pack_kernel, (key_vectors, value_vectors), (pair_sent,), [pltpu.SemaphoreType.DMA((2,))], 0, (0, 1)
    )[0]
    own = call("settle", settle_kernel, (own,), (pair_sent,), [], 1 << 33, (), (), {0: 0})[0]
    line = lax.ppermute(own, "ctx", to_line)
    q, g = queries, grad_out
    own_e, own_stat, own_o, bias, gt, dp = call(
        "own_forward", own_kernel, (docs, q, g, own),
        (e_shape, stat_shape, out_shape, shape((3, rows, rows), f32), shape((heads, dim, rows), bf16), shape((heads, rows, rows), f32)),
        [pltpu.VMEM((rows, rows), f32), *ahead], work,
    )
    line, own_stat = lax.optimization_barrier((line, own_stat))
    side = lax.ppermute(own, "ctx", to_side)
    mate = lax.ppermute(line, "ctx", to_mate)

    def first(name, role, kv):
        return call(
            name, lambda *refs: next_kernel(role, *refs), (docs, q, kv, bias, gt), (e_shape, stat_shape, out_shape), ahead, work
        )

    line_e, line_stat, line_o = first("line_forward", LINE, line)
    side_e, side_stat, side_o = first("side_forward", SIDE, side)
    mate_o, mate_part, early_part, gq, scales, delta = call(
        "rest_forward", rest_kernel,
        (docs, q, g, mate, side, bias, gt, own_stat, line_stat, side_stat, side_e),
        (out_shape, pair_sent, pair_sent, out_shape, shape((4, heads, rows), f32), shape((heads, rows), f32)),
        [*ahead, buffer(e_shape), buffer(stat_shape), *back],
        work,
    )
    mate_back = lax.ppermute(mate_part, "ctx", to_mate)
    line_part, gq = call(
        "line_backward", line_kernel, (docs, q, g, line, line_e, scales, delta, gq), (pair, out_shape), back, work
    )
    line_part = call("line_add", line_add_kernel, (line_part, mate_back), (pair_sent,), [], 0)[0]
    line_part, gq = lax.optimization_barrier((line_part, gq))
    side_part, gq = call(
        "side_backward", side_kernel, (docs, q, g, side, side_e, scales, delta, gq, early_part), (pair_sent, out_shape), back, work
    )
    side_far = lax.ppermute(side_part, "ctx", three_back(count))
    side_near = lax.ppermute(side_part, "ctx", to_mate)
    line_back = lax.ppermute(line_part, "ctx", flip(to_line))
    own_part, grad_query, attended = call(
        "own_backward", last_kernel, (q, g, own, own_e, scales, delta, gq, dp, own_o, mate_o, line_o, side_o), (pair, wide, wide),
        [*back, buffer(wide), buffer(wide), pltpu.SemaphoreType.DMA((2,))], work, (), (1, 2),
    )
    total = call("line_sum", line_sum_kernel, (own_part, line_back), (pair,), [], work)[0]
    narrow = shape((rows, dim), bf16)
    grad_key, grad_value = call("side_sum", side_sum_kernel, (total, side_near, side_far), (narrow, narrow), [], 0)
    return attended, grad_query, grad_key, grad_value


def solution(mesh):
    return jax.shard_map(
        body,
        mesh=mesh,
        in_specs=(P("ctx", "head"), P("ctx", "head"), P("ctx", "head"), P(), P("ctx", "head")),
        out_specs=(P("ctx", "head"), P("ctx", "head"), P("ctx", "head"), P("ctx", "head")),
        check_vma=False,
    )
```

```python
import jax
import jax.numpy as jnp
from jax import lax
from jax.experimental import pallas as pl
from jax.experimental.pallas import tpu as pltpu
from jax.sharding import PartitionSpec as P

LANES = 128
LOG2_E = 1.4426950408889634
MASKED = -1e30

OWN, MATE, LINE, SIDE = range(4)


def nt(a, b):
    return lax.dot_general(a, b, (((1,), (1,)), ((), ())), preferred_element_type=jnp.float32)


def nn(a, b):
    return lax.dot_general(a, b, (((1,), (0,)), ((), ())), preferred_element_type=jnp.float32)


def place(role, rows):
    here, count = lax.axis_index("ctx"), lax.axis_size("ctx")
    odd = lax.rem(here, 2)
    block = here - (0, 1 + 2 * odd, 2, 3 - 2 * odd)[role]
    steps = rows // LANES
    return here * steps, lax.rem(block + count, count) * steps, block >= 0


def find_seen(role, doc_ref, rows):
    mine, at, valid = place(role, rows)
    first = jnp.min(doc_ref[pl.ds(mine, 1), :].astype(jnp.float32))
    last = jnp.max(doc_ref[pl.ds(at + rows // LANES - 1, 1), :].astype(jnp.float32))
    return valid & (first == last)


def is_seen(role, seen_ref):
    return seen_ref[role : role + 1, :][0, 0] > 0


def mask_bias(role, doc_ref, bias):
    rows = bias.shape[0]
    steps = rows // LANES
    mine, at, valid = place(role, rows)
    own_doc = jnp.concatenate([doc_ref[pl.ds(mine + i, 1), :] for i in range(steps)], axis=1)
    for i in range(steps):
        row = jnp.where(valid, doc_ref[pl.ds(at + i, 1), :], -1)
        column = jnp.transpose(jnp.broadcast_to(row, (LANES, LANES)).astype(jnp.float32)).astype(jnp.int32)
        same = jnp.concatenate([column] * steps, axis=1) == own_doc
        if role == OWN:
            key_at = lax.broadcasted_iota(jnp.int32, (LANES, rows), 0) + i * LANES
            same = same & (key_at <= lax.broadcasted_iota(jnp.int32, (LANES, rows), 1))
        bias[i * LANES : (i + 1) * LANES, :] = jnp.where(same, 0.0, MASKED)


def forward(q_ref, kv_ref, bias, gt_ref, e_ref, stat_ref, out_ref, s_ref, vt_ref):
    dim = kv_ref.shape[1] // 2
    heads = q_ref.shape[1] // dim
    factor = dim**-0.5 * LOG2_E
    vt_ref[...] = jnp.transpose(kv_ref[:, dim:])
    for h in range(heads):
        s_ref[h] = nt(kv_ref[:, :dim], q_ref[:, h * dim : (h + 1) * dim])
    for h in range(heads):
        s = s_ref[h] * factor + bias[...]
        top = jnp.max(s, axis=0, keepdims=True)
        e = jnp.exp2(s - top)
        e_ref[h] = e.astype(jnp.bfloat16)
        stat_ref[h : h + 1, :] = top
        stat_ref[heads + h : heads + h + 1, :] = jnp.sum(e, axis=0, keepdims=True)
    for h in range(heads):
        out = nn(vt_ref[...], e_ref[h])
        out_ref[h] = out
        stat_ref[2 * heads + h : 2 * heads + h + 1, :] = jnp.sum(out * gt_ref[h].astype(jnp.float32), axis=0, keepdims=True)


def forward_unseen(stat_ref, out_ref):
    heads = out_ref.shape[0]
    stat_ref[:heads, :] = jnp.full((heads, stat_ref.shape[1]), MASKED, jnp.float32)
    stat_ref[heads:, :] = jnp.zeros((2 * heads, stat_ref.shape[1]), jnp.float32)
    out_ref[...] = jnp.zeros(out_ref.shape, out_ref.dtype)


def backward_queries(g_ref, kv_ref, e_ref, scale_ref, delta_ref, gq_out, kt_ref, p_ref, ds_ref, dp=None):
    dim = kv_ref.shape[1] // 2
    heads = g_ref.shape[1] // dim
    kt_ref[...] = jnp.transpose(kv_ref[:, :dim])
    for h in range(heads):
        probs = e_ref[h] * scale_ref[h : h + 1, :].astype(jnp.bfloat16)
        p_ref[h] = probs
        grad_p = nt(kv_ref[:, dim:], g_ref[:, h * dim : (h + 1) * dim]) if dp is None else dp[h]
        ds_ref[h] = probs * (grad_p - delta_ref[h : h + 1, :]).astype(jnp.bfloat16)
    for h in range(heads):
        gq_out(h, nn(kt_ref[...], ds_ref[h]))


def backward_keys(q_ref, g_ref, p_ref, ds_ref, part_ref):
    dim = part_ref.shape[1] // 2
    cols = [slice(h * dim, (h + 1) * dim) for h in range(q_ref.shape[1] // dim)]
    grad_v = sum(nn(p_ref[h], g_ref[:, c]) for h, c in enumerate(cols))
    part_ref[:, dim:] = grad_v.astype(part_ref.dtype)
    grad_k = sum(nn(ds_ref[h], q_ref[:, c]) for h, c in enumerate(cols))
    part_ref[:, :dim] = (grad_k * dim**-0.5).astype(part_ref.dtype)


def backward_unseen(part_ref, gq_in, gq_ref):
    part_ref[...] = jnp.zeros(part_ref.shape, part_ref.dtype)
    gq_ref[...] = jnp.zeros(gq_ref.shape, gq_ref.dtype) if gq_in is None else gq_in[...]


def pack_kernel(k_ref, v_ref, kv_ref, sems):
    dim = k_ref.shape[1]
    copies = [
        pltpu.make_async_copy(ref, kv_ref.at[:, i * dim : (i + 1) * dim], sems.at[i]) for i, ref in enumerate((k_ref, v_ref))
    ]
    for copy in copies:
        copy.start()
    for copy in copies:
        copy.wait()


def settle_kernel(in_ref, out_ref):
    out_ref[:16, :] = in_ref[:16, :]


def own_kernel(doc_ref, q_ref, g_ref, kv_ref, e_ref, stat_ref, out_ref, bias_ref, gt_ref, dp_ref, seen_ref, bias, s_ref, vt_ref):
    dim = kv_ref.shape[1] // 2
    heads = q_ref.shape[1] // dim
    mask_bias(OWN, doc_ref, bias)
    for h in range(heads):
        gt_ref[h] = jnp.transpose(g_ref[:, h * dim : (h + 1) * dim])
    forward(q_ref, kv_ref, bias, gt_ref, e_ref, stat_ref, out_ref, s_ref, vt_ref)
    for role in (MATE, LINE, SIDE):
        mask_bias(role, doc_ref, bias_ref.at[role - 1])
        seen = find_seen(role, doc_ref, kv_ref.shape[0]).astype(jnp.int32)
        seen_ref[role : role + 1, :] = jnp.full((1, LANES), seen, jnp.int32)
    for h in range(heads):
        dp_ref[h] = nt(kv_ref[:, dim:], g_ref[:, h * dim : (h + 1) * dim])


def next_kernel(role, seen_ref, q_ref, kv_ref, bias_ref, gt_ref, e_ref, stat_ref, out_ref, s_ref, vt_ref):
    seen = is_seen(role, seen_ref)

    @pl.when(seen)
    def _():
        forward(q_ref, kv_ref, bias_ref.at[role - 1], gt_ref, e_ref, stat_ref, out_ref, s_ref, vt_ref)

    @pl.when(jnp.logical_not(seen))
    def _():
        forward_unseen(stat_ref, out_ref)


def next_backward(seen, q_ref, g_ref, kv_ref, e_ref, scale_ref, delta_ref, gq_in, part_ref, gq_ref, kt_ref, p_ref, ds_ref):
    def run():
        def put(h, value):
            gq_ref[h] = value if gq_in is None else gq_in[h] + value

        backward_queries(g_ref, kv_ref, e_ref, scale_ref, delta_ref, put, kt_ref, p_ref, ds_ref)
        backward_keys(q_ref, g_ref, p_ref, ds_ref, part_ref)

    if seen is True:
        run()
        return
    pl.when(seen)(run)

    @pl.when(jnp.logical_not(seen))
    def _():
        backward_unseen(part_ref, gq_in, gq_ref)


def rest_kernel(
    seen_ref, q_ref, g_ref, mate_ref, side_ref, bias_ref, gt_ref, own_stat, line_stat, side_stat, side_e,
    mate_o, mate_part, side_part, gq_part, scale_ref, delta_ref,
    s_ref, vt_ref, mate_e, mate_stat, kt_ref, p_ref, ds_ref,
):
    dim = mate_ref.shape[1] // 2
    heads = q_ref.shape[1] // dim
    next_kernel(MATE, seen_ref, q_ref, mate_ref, bias_ref, gt_ref, mate_e, mate_stat, mate_o, s_ref, vt_ref)
    stats = (own_stat, mate_stat, line_stat, side_stat)
    tops = [ref[:heads, :] for ref in stats]
    top = jnp.maximum(jnp.maximum(tops[0], tops[1]), jnp.maximum(tops[2], tops[3]))
    parts = [jnp.exp2(t - top) for t in tops]
    inverse = 1.0 / sum(p * ref[heads : 2 * heads, :] for p, ref in zip(parts, stats))
    for b in range(4):
        scale_ref[b] = parts[b] * inverse
    delta_ref[...] = sum(p * ref[2 * heads :, :] for p, ref in zip(parts, stats)) * inverse
    rows = mate_ref.shape[0]
    seen = is_seen(MATE, seen_ref)

    @pl.when(seen)
    def _():
        next_backward(
            True, q_ref, g_ref, mate_ref, mate_e, scale_ref.at[MATE], delta_ref, None, mate_part, gq_part, kt_ref, p_ref, ds_ref
        )

    @pl.when(jnp.logical_not(seen))
    def _():
        mate_part[...] = jnp.zeros(mate_part.shape, mate_part.dtype)
        next_backward(
            is_seen(SIDE, seen_ref), q_ref, g_ref, side_ref, side_e, scale_ref.at[SIDE], delta_ref, None,
            side_part, gq_part, kt_ref, p_ref, ds_ref,
        )


def line_kernel(seen_ref, q_ref, g_ref, kv_ref, e_ref, scale_ref, delta_ref, gq_in, part_ref, gq_ref, kt_ref, p_ref, ds_ref):
    next_backward(
        is_seen(LINE, seen_ref), q_ref, g_ref, kv_ref, e_ref, scale_ref.at[LINE], delta_ref, gq_in,
        part_ref, gq_ref, kt_ref, p_ref, ds_ref,
    )


def side_kernel(
    seen_ref, q_ref, g_ref, kv_ref, e_ref, scale_ref, delta_ref, gq_in, early_part, part_ref, gq_ref, kt_ref, p_ref, ds_ref
):
    rows = kv_ref.shape[0]
    late = is_seen(MATE, seen_ref)

    @pl.when(late)
    def _():
        next_backward(
            is_seen(SIDE, seen_ref), q_ref, g_ref, kv_ref, e_ref, scale_ref.at[SIDE], delta_ref, gq_in,
            part_ref, gq_ref, kt_ref, p_ref, ds_ref,
        )

    @pl.when(jnp.logical_not(late))
    def _():
        part_ref[...] = early_part[...]
        gq_ref[...] = gq_in[...]


def turn(h, value, buf):
    buf[:, h * value.shape[0] : (h + 1) * value.shape[0]] = jnp.transpose(value.astype(jnp.bfloat16))


def last_kernel(
    q_ref, g_ref, kv_ref, e_ref, scale_ref, delta_ref, gq_in, dp_ref, own_o, mate_o, line_o, side_o, part_ref, gq_ref, att_ref,
    kt_ref, p_ref, ds_ref, buf, att_buf, sems,
):
    factor = (kv_ref.shape[1] // 2) ** -0.5
    for h in range(own_o.shape[0]):
        out = sum(ref[h] * scale_ref[b, h : h + 1, :] for b, ref in enumerate((own_o, mate_o, line_o, side_o)))
        turn(h, out, att_buf)
    att_copy = pltpu.make_async_copy(att_buf, att_ref, sems.at[0])
    gq_copy = pltpu.make_async_copy(buf, gq_ref, sems.at[1])
    att_copy.start()

    @pl.when(lax.axis_index("ctx") >= 0)
    def _():
        backward_queries(
            g_ref, kv_ref, e_ref, scale_ref.at[OWN], delta_ref, lambda h, v: turn(h, (gq_in[h] + v) * factor, buf),
            kt_ref, p_ref, ds_ref, dp_ref,
        )

    gq_copy.start()

    @pl.when(lax.axis_index("ctx") >= 0)
    def _():
        backward_keys(q_ref, g_ref, p_ref, ds_ref, part_ref)

    att_copy.wait()
    gq_copy.wait()


def line_add_kernel(line_ref, mate_ref, out_ref):
    out_ref[...] = (line_ref[...] + mate_ref[...].astype(jnp.float32)).astype(jnp.bfloat16)


def line_sum_kernel(own_ref, line_ref, out_ref):
    out_ref[...] = own_ref[...] + line_ref[...].astype(jnp.float32)


def side_sum_kernel(sum_ref, near_ref, far_ref, k_ref, v_ref):
    here, count = lax.axis_index("ctx"), lax.axis_size("ctx")
    dim = k_ref.shape[1]
    even = lax.rem(here, 2) == 0
    side = jnp.where(even, near_ref[...].astype(jnp.float32), far_ref[...].astype(jnp.float32))
    total = sum_ref[...] + jnp.where(even | (here + 3 < count), side, 0.0)
    k_ref[...] = total[:, :dim].astype(jnp.bfloat16)
    v_ref[...] = total[:, dim:].astype(jnp.bfloat16)


def call(name, kernel, args, outs, scratch, flops, far_in=(), far_out=(), aliases=None):
    near, far = pl.BlockSpec(memory_space=pltpu.VMEM), pl.BlockSpec(memory_space=pltpu.HBM)
    args = [pltpu.with_memory_space_constraint(a, pltpu.HBM) if i in far_in else a for i, a in enumerate(args)]
    return pl.pallas_call(
        kernel,
        name=name,
        out_shape=outs,
        in_specs=[far if i in far_in else near for i in range(len(args))],
        out_specs=[far if i in far_out else near for i in range(len(outs))],
        scratch_shapes=scratch,
        input_output_aliases=aliases or {},
        cost_estimate=pl.CostEstimate(flops=flops, bytes_accessed=0, transcendentals=0),
        compiler_params=pltpu.CompilerParams(vmem_limit_bytes=16 << 20),
    )(*args)


def three_back(count):
    to = {i: i - 3 for i in range(4, count, 2)}
    to.update({i: i + 3 for i in range(3, count - 3, 2)})
    to.update({0: 2, 1: 0, 2: 4, count - 3: count - 1, count - 1: count - 3})
    return list(to.items())


def body(queries, key_vectors, value_vectors, doc_ids, grad_out):
    rows, dim = key_vectors.shape
    heads = queries.shape[1] // dim
    count = lax.axis_size("ctx")
    to_mate = [(i, i ^ 1) for i in range(count)]
    to_line = [(i, (i + 2) % count) for i in range(count)]
    to_side = [(i, (i + 1 + 2 * (i % 2)) % count) for i in range(count)]
    flip = lambda pairs: [(b, a) for a, b in pairs]
    f32, bf16 = jnp.float32, jnp.bfloat16
    shape = jax.ShapeDtypeStruct
    e_shape, stat_shape, out_shape = shape((heads, rows, rows), bf16), shape((3 * heads, rows), f32), shape((heads, dim, rows), f32)
    pair, pair_sent = shape((rows, 2 * dim), f32), shape((rows, 2 * dim), bf16)
    wide = shape(queries.shape, bf16)
    buffer = lambda like: pltpu.VMEM(like.shape, like.dtype)
    flat = pltpu.VMEM((dim, rows), bf16)
    ahead = [pltpu.VMEM((heads, rows, rows), f32), flat]
    back = [flat, buffer(e_shape), buffer(e_shape)]
    work = heads * rows

    docs = doc_ids.reshape(-1, LANES)
    own = call(
        "pack", pack_kernel, (key_vectors, value_vectors), (pair_sent,), [pltpu.SemaphoreType.DMA((2,))], 0, (0, 1)
    )[0]
    own = call("settle", settle_kernel, (own,), (pair_sent,), [], 1 << 33, (), (), {0: 0})[0]
    line = lax.ppermute(own, "ctx", to_line)
    q, g = queries, grad_out
    own_e, own_stat, own_o, bias, gt, dp, seen = call(
        "own_forward", own_kernel, (docs, q, g, own),
        (e_shape, stat_shape, out_shape, shape((3, rows, rows), f32), shape((heads, dim, rows), bf16), shape((heads, rows, rows), f32),
         shape((8, LANES), jnp.int32)),
        [pltpu.VMEM((rows, rows), f32), *ahead], work,
    )
    line, own_stat = lax.optimization_barrier((line, own_stat))
    side = lax.ppermute(own, "ctx", to_side)
    mate = lax.ppermute(line, "ctx", to_mate)

    def first(name, role, kv):
        return call(
            name, lambda *refs: next_kernel(role, *refs), (seen, q, kv, bias, gt), (e_shape, stat_shape, out_shape), ahead, work
        )

    line_e, line_stat, line_o = first("line_forward", LINE, line)
    side_e, side_stat, side_o = first("side_forward", SIDE, side)
    mate_o, mate_part, early_part, gq, scales, delta = call(
        "rest_forward", rest_kernel,
        (seen, q, g, mate, side, bias, gt, own_stat, line_stat, side_stat, side_e),
        (out_shape, pair_sent, pair_sent, out_shape, shape((4, heads, rows), f32), shape((heads, rows), f32)),
        [*ahead, buffer(e_shape), buffer(stat_shape), *back],
        work,
    )
    mate_back = lax.ppermute(mate_part, "ctx", to_mate)
    line_part, gq = call(
        "line_backward", line_kernel, (seen, q, g, line, line_e, scales, delta, gq), (pair, out_shape), back, work
    )
    line_part = call("line_add", line_add_kernel, (line_part, mate_back), (pair_sent,), [], 0)[0]
    line_part, gq = lax.optimization_barrier((line_part, gq))
    side_part, gq = call(
        "side_backward", side_kernel, (seen, q, g, side, side_e, scales, delta, gq, early_part), (pair_sent, out_shape), back, work
    )
    side_far = lax.ppermute(side_part, "ctx", three_back(count))
    side_near = lax.ppermute(side_part, "ctx", to_mate)
    line_back = lax.ppermute(line_part, "ctx", flip(to_line))
    own_part, grad_query, attended = call(
        "own_backward", last_kernel, (q, g, own, own_e, scales, delta, gq, dp, own_o, mate_o, line_o, side_o), (pair, wide, wide),
        [*back, buffer(wide), buffer(wide), pltpu.SemaphoreType.DMA((2,))], work, (), (1, 2),
    )
    total = call("line_sum", line_sum_kernel, (own_part, line_back), (pair,), [], work)[0]
    narrow = shape((rows, dim), bf16)
    grad_key, grad_value = call("side_sum", side_sum_kernel, (total, side_near, side_far), (narrow, narrow), [], 0)
    return attended, grad_query, grad_key, grad_value


def solution(mesh):
    return jax.shard_map(
        body,
        mesh=mesh,
        in_specs=(P("ctx", "head"), P("ctx", "head"), P("ctx", "head"), P(), P("ctx", "head")),
        out_specs=(P("ctx", "head"), P("ctx", "head"), P("ctx", "head"), P("ctx", "head")),
        check_vma=False,
    )
```

```python
import jax
import jax.numpy as jnp
from jax import lax
from jax.experimental import pallas as pl
from jax.experimental.pallas import tpu as pltpu
from jax.sharding import PartitionSpec as P

LANES = 128
LOG2_E = 1.4426950408889634
MASKED = -1e30

OWN, MATE, LINE, SIDE = range(4)


def nt(a, b):
    return lax.dot_general(a, b, (((1,), (1,)), ((), ())), preferred_element_type=jnp.float32)


def nn(a, b):
    return lax.dot_general(a, b, (((1,), (0,)), ((), ())), preferred_element_type=jnp.float32)


def place(role, rows):
    here, count = lax.axis_index("ctx"), lax.axis_size("ctx")
    odd = lax.rem(here, 2)
    block = here - (0, 1 + 2 * odd, 2, 3 - 2 * odd)[role]
    steps = rows // LANES
    return here * steps, lax.rem(block + count, count) * steps, block >= 0


def find_seen(role, doc_ref, rows):
    mine, at, valid = place(role, rows)
    first = jnp.min(doc_ref[pl.ds(mine, 1), :].astype(jnp.float32))
    last = jnp.max(doc_ref[pl.ds(at + rows // LANES - 1, 1), :].astype(jnp.float32))
    return valid & (first == last)


def is_seen(role, seen_ref):
    return seen_ref[role : role + 1, :][0, 0] > 0


def mask_bias(role, doc_ref, bias):
    rows = bias.shape[0]
    steps = rows // LANES
    mine, at, valid = place(role, rows)
    own_doc = jnp.concatenate([doc_ref[pl.ds(mine + i, 1), :] for i in range(steps)], axis=1)
    for i in range(steps):
        row = jnp.where(valid, doc_ref[pl.ds(at + i, 1), :], -1)
        column = jnp.transpose(jnp.broadcast_to(row, (LANES, LANES)).astype(jnp.float32)).astype(jnp.int32)
        same = jnp.concatenate([column] * steps, axis=1) == own_doc
        if role == OWN:
            key_at = lax.broadcasted_iota(jnp.int32, (LANES, rows), 0) + i * LANES
            same = same & (key_at <= lax.broadcasted_iota(jnp.int32, (LANES, rows), 1))
        bias[i * LANES : (i + 1) * LANES, :] = jnp.where(same, 0.0, MASKED)


def forward(q_ref, kv_ref, bias, gt_ref, e_ref, stat_ref, out_ref, s_ref, vt_ref):
    dim = kv_ref.shape[1] // 2
    heads = q_ref.shape[1] // dim
    factor = dim**-0.5 * LOG2_E
    vt_ref[...] = jnp.transpose(kv_ref[:, dim:])
    for h in range(heads):
        s_ref[h] = nt(kv_ref[:, :dim], q_ref[:, h * dim : (h + 1) * dim])
    for h in range(heads):
        s = s_ref[h] * factor + bias[...]
        top = jnp.max(s, axis=0, keepdims=True)
        e = jnp.exp2(s - top)
        e_ref[h] = e.astype(jnp.bfloat16)
        stat_ref[h : h + 1, :] = top
        stat_ref[heads + h : heads + h + 1, :] = jnp.sum(e, axis=0, keepdims=True)
    for h in range(heads):
        out = nn(vt_ref[...], e_ref[h])
        out_ref[h] = out
        stat_ref[2 * heads + h : 2 * heads + h + 1, :] = jnp.sum(out * gt_ref[h].astype(jnp.float32), axis=0, keepdims=True)


def forward_unseen(stat_ref, out_ref):
    heads = out_ref.shape[0]
    stat_ref[:heads, :] = jnp.full((heads, stat_ref.shape[1]), MASKED, jnp.float32)
    stat_ref[heads:, :] = jnp.zeros((2 * heads, stat_ref.shape[1]), jnp.float32)
    out_ref[...] = jnp.zeros(out_ref.shape, out_ref.dtype)


def backward_queries(g_ref, kv_ref, e_ref, scale_ref, delta_ref, gq_out, kt_ref, p_ref, ds_ref, dp=None):
    dim = kv_ref.shape[1] // 2
    heads = g_ref.shape[1] // dim
    kt_ref[...] = jnp.transpose(kv_ref[:, :dim])
    for h in range(heads):
        probs = e_ref[h] * scale_ref[h : h + 1, :].astype(jnp.bfloat16)
        p_ref[h] = probs
        grad_p = nt(kv_ref[:, dim:], g_ref[:, h * dim : (h + 1) * dim]) if dp is None else dp[h]
        ds_ref[h] = probs * (grad_p - delta_ref[h : h + 1, :]).astype(jnp.bfloat16)
    for h in range(heads):
        gq_out(h, nn(kt_ref[...], ds_ref[h]))


def backward_keys(q_ref, g_ref, p_ref, ds_ref, part_ref):
    dim = part_ref.shape[1] // 2
    cols = [slice(h * dim, (h + 1) * dim) for h in range(q_ref.shape[1] // dim)]
    grad_v = sum(nn(p_ref[h], g_ref[:, c]) for h, c in enumerate(cols))
    part_ref[:, dim:] = grad_v.astype(part_ref.dtype)
    grad_k = sum(nn(ds_ref[h], q_ref[:, c]) for h, c in enumerate(cols))
    part_ref[:, :dim] = (grad_k * dim**-0.5).astype(part_ref.dtype)


def backward_unseen(part_ref, gq_in, gq_ref):
    part_ref[...] = jnp.zeros(part_ref.shape, part_ref.dtype)
    gq_ref[...] = jnp.zeros(gq_ref.shape, gq_ref.dtype) if gq_in is None else gq_in[...]


def pack_kernel(k_ref, v_ref, kv_ref, sems):
    dim = k_ref.shape[1]
    copies = [
        pltpu.make_async_copy(ref, kv_ref.at[:, i * dim : (i + 1) * dim], sems.at[i]) for i, ref in enumerate((k_ref, v_ref))
    ]
    for copy in copies:
        copy.start()
    for copy in copies:
        copy.wait()


def settle_kernel(in_ref, out_ref):
    out_ref[:16, :] = in_ref[:16, :]


def own_kernel(doc_ref, q_ref, g_ref, kv_ref, e_ref, stat_ref, out_ref, bias_ref, gt_ref, dp_ref, seen_ref, bias, s_ref, vt_ref):
    dim = kv_ref.shape[1] // 2
    heads = q_ref.shape[1] // dim
    mask_bias(OWN, doc_ref, bias)
    for h in range(heads):
        gt_ref[h] = jnp.transpose(g_ref[:, h * dim : (h + 1) * dim])
    forward(q_ref, kv_ref, bias, gt_ref, e_ref, stat_ref, out_ref, s_ref, vt_ref)
    for role in (MATE, LINE, SIDE):
        mask_bias(role, doc_ref, bias_ref.at[role - 1])
        seen = find_seen(role, doc_ref, kv_ref.shape[0]).astype(jnp.int32)
        seen_ref[role : role + 1, :] = jnp.full((1, LANES), seen, jnp.int32)
    for h in range(heads):
        dp_ref[h] = nt(kv_ref[:, dim:], g_ref[:, h * dim : (h + 1) * dim])


def next_kernel(role, seen_ref, q_ref, kv_ref, bias_ref, gt_ref, e_ref, stat_ref, out_ref, s_ref, vt_ref):
    seen = is_seen(role, seen_ref)

    @pl.when(seen)
    def _():
        forward(q_ref, kv_ref, bias_ref.at[role - 1], gt_ref, e_ref, stat_ref, out_ref, s_ref, vt_ref)

    @pl.when(jnp.logical_not(seen))
    def _():
        forward_unseen(stat_ref, out_ref)


def next_backward(seen, q_ref, g_ref, kv_ref, e_ref, scale_ref, delta_ref, gq_in, part_ref, gq_ref, kt_ref, p_ref, ds_ref):
    def run():
        def put(h, value):
            gq_ref[h] = value if gq_in is None else gq_in[h] + value

        backward_queries(g_ref, kv_ref, e_ref, scale_ref, delta_ref, put, kt_ref, p_ref, ds_ref)
        backward_keys(q_ref, g_ref, p_ref, ds_ref, part_ref)

    if seen is True:
        run()
        return
    pl.when(seen)(run)

    @pl.when(jnp.logical_not(seen))
    def _():
        backward_unseen(part_ref, gq_in, gq_ref)


def rest_kernel(
    seen_ref, q_ref, g_ref, mate_ref, side_ref, bias_ref, gt_ref, own_stat, line_stat, side_stat, side_e,
    mate_o, mate_part, side_part, gq_part, scale_ref, delta_ref,
    s_ref, vt_ref, mate_e, mate_stat, kt_ref, p_ref, ds_ref,
):
    dim = mate_ref.shape[1] // 2
    heads = q_ref.shape[1] // dim
    next_kernel(MATE, seen_ref, q_ref, mate_ref, bias_ref, gt_ref, mate_e, mate_stat, mate_o, s_ref, vt_ref)
    stats = (own_stat, mate_stat, line_stat, side_stat)
    tops = [ref[:heads, :] for ref in stats]
    top = jnp.maximum(jnp.maximum(tops[0], tops[1]), jnp.maximum(tops[2], tops[3]))
    parts = [jnp.exp2(t - top) for t in tops]
    inverse = 1.0 / sum(p * ref[heads : 2 * heads, :] for p, ref in zip(parts, stats))
    for b in range(4):
        scale_ref[b] = parts[b] * inverse
    delta_ref[...] = sum(p * ref[2 * heads :, :] for p, ref in zip(parts, stats)) * inverse
    rows = mate_ref.shape[0]
    seen = is_seen(MATE, seen_ref)

    @pl.when(seen)
    def _():
        next_backward(
            True, q_ref, g_ref, mate_ref, mate_e, scale_ref.at[MATE], delta_ref, None, mate_part, gq_part, kt_ref, p_ref, ds_ref
        )

    @pl.when(jnp.logical_not(seen))
    def _():
        mate_part[...] = jnp.zeros(mate_part.shape, mate_part.dtype)
        next_backward(
            is_seen(SIDE, seen_ref), q_ref, g_ref, side_ref, side_e, scale_ref.at[SIDE], delta_ref, None,
            side_part, gq_part, kt_ref, p_ref, ds_ref,
        )


def line_kernel(seen_ref, q_ref, g_ref, kv_ref, e_ref, scale_ref, delta_ref, gq_in, part_ref, gq_ref, kt_ref, p_ref, ds_ref):
    next_backward(
        is_seen(LINE, seen_ref), q_ref, g_ref, kv_ref, e_ref, scale_ref.at[LINE], delta_ref, gq_in,
        part_ref, gq_ref, kt_ref, p_ref, ds_ref,
    )


def side_kernel(
    seen_ref, q_ref, g_ref, kv_ref, e_ref, scale_ref, delta_ref, gq_in, early_part, line_part,
    part_ref, near_ref, gq_ref, kt_ref, p_ref, ds_ref,
):
    late = is_seen(MATE, seen_ref)

    @pl.when(late)
    def _():
        next_backward(
            is_seen(SIDE, seen_ref), q_ref, g_ref, kv_ref, e_ref, scale_ref.at[SIDE], delta_ref, gq_in,
            part_ref, gq_ref, kt_ref, p_ref, ds_ref,
        )

    @pl.when(jnp.logical_not(late))
    def _():
        part_ref[...] = early_part[...]
        gq_ref[...] = gq_in[...]

    joint = is_joint(lax.axis_index("ctx") // 2, lax.axis_size("ctx") // 2)
    near_ref[...] = jnp.where(joint, line_part[...], part_ref[...])


def turn(h, value, buf):
    buf[:, h * value.shape[0] : (h + 1) * value.shape[0]] = jnp.transpose(value.astype(jnp.bfloat16))


def last_kernel(
    q_ref, g_ref, kv_ref, e_ref, scale_ref, delta_ref, gq_in, dp_ref, own_o, mate_o, line_o, side_o, part_ref, gq_ref, att_ref,
    kt_ref, p_ref, ds_ref, buf, att_buf, sems,
):
    factor = (kv_ref.shape[1] // 2) ** -0.5
    for h in range(own_o.shape[0]):
        out = sum(ref[h] * scale_ref[b, h : h + 1, :] for b, ref in enumerate((own_o, mate_o, line_o, side_o)))
        turn(h, out, att_buf)
    att_copy = pltpu.make_async_copy(att_buf, att_ref, sems.at[0])
    gq_copy = pltpu.make_async_copy(buf, gq_ref, sems.at[1])
    att_copy.start()

    @pl.when(lax.axis_index("ctx") >= 0)
    def _():
        backward_queries(
            g_ref, kv_ref, e_ref, scale_ref.at[OWN], delta_ref, lambda h, v: turn(h, (gq_in[h] + v) * factor, buf),
            kt_ref, p_ref, ds_ref, dp_ref,
        )

    gq_copy.start()

    @pl.when(lax.axis_index("ctx") >= 0)
    def _():
        backward_keys(q_ref, g_ref, p_ref, ds_ref, part_ref)

    att_copy.wait()
    gq_copy.wait()


def line_add_kernel(line_ref, mate_ref, out_ref):
    out_ref[...] = (line_ref[...] + mate_ref[...].astype(jnp.float32)).astype(jnp.bfloat16)


def line_sum_kernel(own_ref, line_ref, out_ref):
    chip, chips = lax.axis_index("ctx") // 2, lax.axis_size("ctx") // 2
    in_ring = (chip < chips - 1) & (chip != chips - SECOND - 1)
    out_ref[...] = own_ref[...] + jnp.where(in_ring, line_ref[...].astype(jnp.float32), 0.0)


def far_sum_kernel(sum_ref, far_ref, out_ref):
    here, count = lax.axis_index("ctx"), lax.axis_size("ctx")
    even = lax.rem(here, 2) == 0
    taken = (even & is_joint(here // 2, count // 2)) | (jnp.logical_not(even) & (here + 3 < count))
    out_ref[...] = sum_ref[...] + jnp.where(taken, far_ref[...].astype(jnp.float32), 0.0)


def near_sum_kernel(sum_ref, near_ref, k_ref, v_ref):
    here, count = lax.axis_index("ctx"), lax.axis_size("ctx")
    chip, dim = here // 2, k_ref.shape[1]
    even, joint = lax.rem(here, 2) == 0, is_joint(chip, count // 2)
    taken = (chip == count // 2 - SECOND - 1) | (jnp.logical_not(joint) & even)
    total = sum_ref[...] + jnp.where(taken, near_ref[...].astype(jnp.float32), 0.0)
    k_ref[...] = total[:, :dim].astype(jnp.bfloat16)
    v_ref[...] = total[:, dim:].astype(jnp.bfloat16)


def call(name, kernel, args, outs, scratch, flops, far_in=(), far_out=(), aliases=None):
    near, far = pl.BlockSpec(memory_space=pltpu.VMEM), pl.BlockSpec(memory_space=pltpu.HBM)
    args = [pltpu.with_memory_space_constraint(a, pltpu.HBM) if i in far_in else a for i, a in enumerate(args)]
    return pl.pallas_call(
        kernel,
        name=name,
        out_shape=outs,
        in_specs=[far if i in far_in else near for i in range(len(args))],
        out_specs=[far if i in far_out else near for i in range(len(outs))],
        scratch_shapes=scratch,
        input_output_aliases=aliases or {},
        cost_estimate=pl.CostEstimate(flops=flops, bytes_accessed=0, transcendentals=0),
        compiler_params=pltpu.CompilerParams(vmem_limit_bytes=16 << 20),
    )(*args)


SECOND = 3


def line_rings(count):
    to = {i: i - 2 for i in range(count)}
    first = count - 2 * SECOND
    to.update({core: first - 2 + core for core in (0, 1)})
    to.update({first + core: count - 2 + core for core in (0, 1)})
    return list(to.items())


def is_joint(chip, chips):
    return (chip == chips - SECOND - 1) | (chip == chips - SECOND)


def near_swaps(count):
    to = {i: i ^ 1 for i in range(count)}
    first = count - 2 * SECOND
    for i in (first - 2, first - 1):
        to[i], to[i + 2] = i + 2, i
    return list(to.items())


def three_back(count):
    to = {i: i - 3 for i in range(4, count, 2)}
    to.update({i: i + 3 for i in range(3, count - 3, 2)})
    to.update({0: 2, 1: 0, 2: 4, count - 3: count - 1, count - 1: count - 3})
    i = count - 2 * SECOND - 1
    to.update({i: i - 1, i + 2: i + 1, i - 4: i + 3, i - 2: i + 5})
    return list(to.items())


def body(queries, key_vectors, value_vectors, doc_ids, grad_out):
    rows, dim = key_vectors.shape
    heads = queries.shape[1] // dim
    count = lax.axis_size("ctx")
    to_mate = [(i, i ^ 1) for i in range(count)]
    to_line = [(i, (i + 2) % count) for i in range(count)]
    to_side = [(i, (i + 1 + 2 * (i % 2)) % count) for i in range(count)]
    f32, bf16 = jnp.float32, jnp.bfloat16
    shape = jax.ShapeDtypeStruct
    e_shape, stat_shape, out_shape = shape((heads, rows, rows), bf16), shape((3 * heads, rows), f32), shape((heads, dim, rows), f32)
    pair, pair_sent = shape((rows, 2 * dim), f32), shape((rows, 2 * dim), bf16)
    wide = shape(queries.shape, bf16)
    buffer = lambda like: pltpu.VMEM(like.shape, like.dtype)
    flat = pltpu.VMEM((dim, rows), bf16)
    ahead = [pltpu.VMEM((heads, rows, rows), f32), flat]
    back = [flat, buffer(e_shape), buffer(e_shape)]
    work = heads * rows

    docs = doc_ids.reshape(-1, LANES)
    own = call(
        "pack", pack_kernel, (key_vectors, value_vectors), (pair_sent,), [pltpu.SemaphoreType.DMA((2,))], 0, (0, 1)
    )[0]
    own = call("settle", settle_kernel, (own,), (pair_sent,), [], 1 << 33, (), (), {0: 0})[0]
    line = lax.ppermute(own, "ctx", to_line)
    q, g = queries, grad_out
    own_e, own_stat, own_o, bias, gt, dp, seen = call(
        "own_forward", own_kernel, (docs, q, g, own),
        (e_shape, stat_shape, out_shape, shape((3, rows, rows), f32), shape((heads, dim, rows), bf16), shape((heads, rows, rows), f32),
         shape((8, LANES), jnp.int32)),
        [pltpu.VMEM((rows, rows), f32), *ahead], work,
    )
    line, own_stat = lax.optimization_barrier((line, own_stat))
    side = lax.ppermute(own, "ctx", to_side)
    mate = lax.ppermute(line, "ctx", to_mate)

    def first(name, role, kv):
        return call(
            name, lambda *refs: next_kernel(role, *refs), (seen, q, kv, bias, gt), (e_shape, stat_shape, out_shape), ahead, work
        )

    line_e, line_stat, line_o = first("line_forward", LINE, line)
    side_e, side_stat, side_o = first("side_forward", SIDE, side)
    mate_o, mate_part, early_part, gq, scales, delta = call(
        "rest_forward", rest_kernel,
        (seen, q, g, mate, side, bias, gt, own_stat, line_stat, side_stat, side_e),
        (out_shape, pair_sent, pair_sent, out_shape, shape((4, heads, rows), f32), shape((heads, rows), f32)),
        [*ahead, buffer(e_shape), buffer(stat_shape), *back],
        work,
    )
    mate_back = lax.ppermute(mate_part, "ctx", to_mate)
    line_part, gq = call(
        "line_backward", line_kernel, (seen, q, g, line, line_e, scales, delta, gq), (pair, out_shape), back, work
    )
    line_part = call("line_add", line_add_kernel, (line_part, mate_back), (pair_sent,), [], 0)[0]
    line_part, gq = lax.optimization_barrier((line_part, gq))
    side_part, near_part, gq = call(
        "side_backward", side_kernel, (seen, q, g, side, side_e, scales, delta, gq, early_part, line_part),
        (pair_sent, pair_sent, out_shape), back, work,
    )
    side_far = lax.ppermute(side_part, "ctx", three_back(count))
    side_near = lax.ppermute(near_part, "ctx", near_swaps(count))
    line_back = lax.ppermute(line_part, "ctx", line_rings(count))
    own_part, grad_query, attended = call(
        "own_backward", last_kernel, (q, g, own, own_e, scales, delta, gq, dp, own_o, mate_o, line_o, side_o), (pair, wide, wide),
        [*back, buffer(wide), buffer(wide), pltpu.SemaphoreType.DMA((2,))], work, (), (1, 2),
    )
    total = call("line_sum", line_sum_kernel, (own_part, line_back), (pair,), [], work)[0]
    narrow = shape((rows, dim), bf16)
    total = call("far_sum", far_sum_kernel, (total, side_far), (pair,), [], work)[0]
    grad_key, grad_value = call("near_sum", near_sum_kernel, (total, side_near), (narrow, narrow), [], 0)
    return attended, grad_query, grad_key, grad_value


def solution(mesh):
    return jax.shard_map(
        body,
        mesh=mesh,
        in_specs=(P("ctx", "head"), P("ctx", "head"), P("ctx", "head"), P(), P("ctx", "head")),
        out_specs=(P("ctx", "head"), P("ctx", "head"), P("ctx", "head"), P("ctx", "head")),
        check_vma=False,
    )
```

```python
import jax
import jax.numpy as jnp
from jax import lax
from jax.experimental import pallas as pl
from jax.experimental.pallas import tpu as pltpu
from jax.sharding import PartitionSpec as P

LANES = 128
LOG2_E = 1.4426950408889634
MASKED = -1e30

OWN, MATE, LINE, SIDE = range(4)


def nt(a, b):
    return lax.dot_general(a, b, (((1,), (1,)), ((), ())), preferred_element_type=jnp.float32)


def nn(a, b):
    return lax.dot_general(a, b, (((1,), (0,)), ((), ())), preferred_element_type=jnp.float32)


def place(role, rows):
    here, count = lax.axis_index("ctx"), lax.axis_size("ctx")
    odd = lax.rem(here, 2)
    block = here - (0, 1 + 2 * odd, 2, 3 - 2 * odd)[role]
    steps = rows // LANES
    return here * steps, lax.rem(block + count, count) * steps, block >= 0


def find_seen(role, doc_ref, rows):
    mine, at, valid = place(role, rows)
    steps = rows // LANES
    first = jnp.min(doc_ref[pl.ds(mine, 1), :].astype(jnp.float32))
    last = jnp.max(doc_ref[pl.ds(at + steps - 1, 1), :].astype(jnp.float32))
    middle = jnp.max(doc_ref[pl.ds(at + steps // 2 - 1, 1), :].astype(jnp.float32))
    level = (last == first).astype(jnp.int32) + (middle == first).astype(jnp.int32)
    return jnp.where(valid, level, 0)


def seen_level(role, seen_ref):
    return seen_ref[role : role + 1, :][0, 0]


def is_seen(role, seen_ref):
    return seen_ref[role : role + 1, :][0, 0] > 0


def mask_bias(role, doc_ref, bias):
    rows = bias.shape[0]
    steps = rows // LANES
    mine, at, valid = place(role, rows)
    own_doc = jnp.concatenate([doc_ref[pl.ds(mine + i, 1), :] for i in range(steps)], axis=1)
    for i in range(steps):
        row = jnp.where(valid, doc_ref[pl.ds(at + i, 1), :], -1)
        column = jnp.transpose(jnp.broadcast_to(row, (LANES, LANES)).astype(jnp.float32)).astype(jnp.int32)
        same = jnp.concatenate([column] * steps, axis=1) == own_doc
        if role == OWN:
            key_at = lax.broadcasted_iota(jnp.int32, (LANES, rows), 0) + i * LANES
            same = same & (key_at <= lax.broadcasted_iota(jnp.int32, (LANES, rows), 1))
        bias[i * LANES : (i + 1) * LANES, :] = jnp.where(same, 0.0, MASKED)


def forward(q_ref, kv_ref, bias, gt_ref, e_ref, stat_ref, out_ref, s_ref, vt_ref, start=0):
    dim = kv_ref.shape[1] // 2
    heads = q_ref.shape[1] // dim
    factor = dim**-0.5 * LOG2_E
    keys = slice(start, kv_ref.shape[0])
    vt_ref[:, keys] = jnp.transpose(kv_ref[keys, dim:])
    for h in range(heads):
        s_ref[h, keys, :] = nt(kv_ref[keys, :dim], q_ref[:, h * dim : (h + 1) * dim])
    for h in range(heads):
        s = s_ref[h, keys, :] * factor + bias[keys, :]
        top = jnp.max(s, axis=0, keepdims=True)
        e = jnp.exp2(s - top)
        e_ref[h, keys, :] = e.astype(jnp.bfloat16)
        stat_ref[h : h + 1, :] = top
        stat_ref[heads + h : heads + h + 1, :] = jnp.sum(e, axis=0, keepdims=True)
    for h in range(heads):
        out = nn(vt_ref[:, keys], e_ref[h, keys, :])
        out_ref[h] = out
        stat_ref[2 * heads + h : 2 * heads + h + 1, :] = jnp.sum(out * gt_ref[h].astype(jnp.float32), axis=0, keepdims=True)


def forward_unseen(stat_ref, out_ref):
    heads = out_ref.shape[0]
    stat_ref[:heads, :] = jnp.full((heads, stat_ref.shape[1]), MASKED, jnp.float32)
    stat_ref[heads:, :] = jnp.zeros((2 * heads, stat_ref.shape[1]), jnp.float32)
    out_ref[...] = jnp.zeros(out_ref.shape, out_ref.dtype)


def backward_queries(g_ref, kv_ref, e_ref, scale_ref, delta_ref, gq_out, kt_ref, p_ref, ds_ref, dp=None, start=0):
    dim = kv_ref.shape[1] // 2
    heads = g_ref.shape[1] // dim
    keys = slice(start, kv_ref.shape[0])
    kt_ref[:, keys] = jnp.transpose(kv_ref[keys, :dim])
    for h in range(heads):
        probs = e_ref[h, keys, :] * scale_ref[h : h + 1, :].astype(jnp.bfloat16)
        p_ref[h, keys, :] = probs
        grad_p = nt(kv_ref[keys, dim:], g_ref[:, h * dim : (h + 1) * dim]) if dp is None else dp[h]
        ds_ref[h, keys, :] = probs * (grad_p - delta_ref[h : h + 1, :]).astype(jnp.bfloat16)
    for h in range(heads):
        gq_out(h, nn(kt_ref[:, keys], ds_ref[h, keys, :]))


def backward_keys(q_ref, g_ref, p_ref, ds_ref, part_ref, start=0):
    rows, dim = part_ref.shape[0], part_ref.shape[1] // 2
    keys = slice(start, rows)
    cols = [slice(h * dim, (h + 1) * dim) for h in range(q_ref.shape[1] // dim)]
    if start:
        part_ref[:start, :] = jnp.zeros((start, 2 * dim), part_ref.dtype)
    grad_v = sum(nn(p_ref[h, keys, :], g_ref[:, c]) for h, c in enumerate(cols))
    part_ref[keys, dim:] = grad_v.astype(part_ref.dtype)
    grad_k = sum(nn(ds_ref[h, keys, :], q_ref[:, c]) for h, c in enumerate(cols))
    part_ref[keys, :dim] = (grad_k * dim**-0.5).astype(part_ref.dtype)


def backward_unseen(part_ref, gq_in, gq_ref):
    part_ref[...] = jnp.zeros(part_ref.shape, part_ref.dtype)
    gq_ref[...] = jnp.zeros(gq_ref.shape, gq_ref.dtype) if gq_in is None else gq_in[...]


def pack_kernel(k_ref, v_ref, kv_ref, sems):
    dim = k_ref.shape[1]
    copies = [
        pltpu.make_async_copy(ref, kv_ref.at[:, i * dim : (i + 1) * dim], sems.at[i]) for i, ref in enumerate((k_ref, v_ref))
    ]
    for copy in copies:
        copy.start()
    for copy in copies:
        copy.wait()


def settle_kernel(in_ref, out_ref):
    out_ref[:16, :] = in_ref[:16, :]


def own_kernel(doc_ref, q_ref, g_ref, kv_ref, e_ref, stat_ref, out_ref, bias_ref, gt_ref, dp_ref, seen_ref, bias, s_ref, vt_ref):
    dim = kv_ref.shape[1] // 2
    heads = q_ref.shape[1] // dim
    mask_bias(OWN, doc_ref, bias)
    for h in range(heads):
        gt_ref[h] = jnp.transpose(g_ref[:, h * dim : (h + 1) * dim])
    forward(q_ref, kv_ref, bias, gt_ref, e_ref, stat_ref, out_ref, s_ref, vt_ref)
    for role in (MATE, LINE, SIDE):
        mask_bias(role, doc_ref, bias_ref.at[role - 1])
        seen = find_seen(role, doc_ref, kv_ref.shape[0])
        seen_ref[role : role + 1, :] = jnp.full((1, LANES), seen, jnp.int32)
    for h in range(heads):
        dp_ref[h] = nt(kv_ref[:, dim:], g_ref[:, h * dim : (h + 1) * dim])


def next_kernel(role, seen_ref, q_ref, kv_ref, bias_ref, gt_ref, e_ref, stat_ref, out_ref, s_ref, vt_ref):
    level = seen_level(role, seen_ref)
    for some, start in ((2, 0), (1, kv_ref.shape[0] // 2)):

        @pl.when(level == some)
        def _():
            forward(q_ref, kv_ref, bias_ref.at[role - 1], gt_ref, e_ref, stat_ref, out_ref, s_ref, vt_ref, start)

    @pl.when(level == 0)
    def _():
        forward_unseen(stat_ref, out_ref)


def next_backward(level, q_ref, g_ref, kv_ref, e_ref, scale_ref, delta_ref, gq_in, part_ref, gq_ref, kt_ref, p_ref, ds_ref):
    def put(h, value):
        gq_ref[h] = value if gq_in is None else gq_in[h] + value

    for some, start in ((2, 0), (1, kv_ref.shape[0] // 2)):

        @pl.when(level == some)
        def _():
            backward_queries(g_ref, kv_ref, e_ref, scale_ref, delta_ref, put, kt_ref, p_ref, ds_ref, None, start)
            backward_keys(q_ref, g_ref, p_ref, ds_ref, part_ref, start)

    @pl.when(level == 0)
    def _():
        backward_unseen(part_ref, gq_in, gq_ref)


def rest_kernel(
    seen_ref, q_ref, g_ref, mate_ref, side_ref, bias_ref, gt_ref, own_stat, line_stat, side_stat, side_e,
    mate_o, mate_part, side_part, gq_part, scale_ref, delta_ref,
    s_ref, vt_ref, mate_e, mate_stat, kt_ref, p_ref, ds_ref,
):
    dim = mate_ref.shape[1] // 2
    heads = q_ref.shape[1] // dim
    next_kernel(MATE, seen_ref, q_ref, mate_ref, bias_ref, gt_ref, mate_e, mate_stat, mate_o, s_ref, vt_ref)
    stats = (own_stat, mate_stat, line_stat, side_stat)
    tops = [ref[:heads, :] for ref in stats]
    top = jnp.maximum(jnp.maximum(tops[0], tops[1]), jnp.maximum(tops[2], tops[3]))
    parts = [jnp.exp2(t - top) for t in tops]
    inverse = 1.0 / sum(p * ref[heads : 2 * heads, :] for p, ref in zip(parts, stats))
    for b in range(4):
        scale_ref[b] = parts[b] * inverse
    delta_ref[...] = sum(p * ref[2 * heads :, :] for p, ref in zip(parts, stats)) * inverse
    rows = mate_ref.shape[0]
    seen = is_seen(MATE, seen_ref)

    @pl.when(seen)
    def _():
        next_backward(
            seen_level(MATE, seen_ref), q_ref, g_ref, mate_ref, mate_e, scale_ref.at[MATE], delta_ref, None, mate_part, gq_part, kt_ref, p_ref, ds_ref
        )

    @pl.when(jnp.logical_not(seen))
    def _():
        mate_part[...] = jnp.zeros(mate_part.shape, mate_part.dtype)
        next_backward(
            seen_level(SIDE, seen_ref), q_ref, g_ref, side_ref, side_e, scale_ref.at[SIDE], delta_ref, None,
            side_part, gq_part, kt_ref, p_ref, ds_ref,
        )


def line_kernel(seen_ref, q_ref, g_ref, kv_ref, e_ref, scale_ref, delta_ref, gq_in, part_ref, gq_ref, kt_ref, p_ref, ds_ref):
    next_backward(
        seen_level(LINE, seen_ref), q_ref, g_ref, kv_ref, e_ref, scale_ref.at[LINE], delta_ref, gq_in,
        part_ref, gq_ref, kt_ref, p_ref, ds_ref,
    )


def side_kernel(
    seen_ref, q_ref, g_ref, kv_ref, e_ref, scale_ref, delta_ref, gq_in, early_part, part_ref, gq_ref, kt_ref, p_ref, ds_ref
):
    rows = kv_ref.shape[0]
    late = is_seen(MATE, seen_ref)

    @pl.when(late)
    def _():
        next_backward(
            seen_level(SIDE, seen_ref), q_ref, g_ref, kv_ref, e_ref, scale_ref.at[SIDE], delta_ref, gq_in,
            part_ref, gq_ref, kt_ref, p_ref, ds_ref,
        )

    @pl.when(jnp.logical_not(late))
    def _():
        part_ref[...] = early_part[...]
        gq_ref[...] = gq_in[...]


def turn(h, value, buf):
    buf[:, h * value.shape[0] : (h + 1) * value.shape[0]] = jnp.transpose(value.astype(jnp.bfloat16))


def last_kernel(
    q_ref, g_ref, kv_ref, e_ref, scale_ref, delta_ref, gq_in, dp_ref, own_o, mate_o, line_o, side_o, part_ref, gq_ref, att_ref,
    kt_ref, p_ref, ds_ref, buf, att_buf, sems,
):
    factor = (kv_ref.shape[1] // 2) ** -0.5
    for h in range(own_o.shape[0]):
        out = sum(ref[h] * scale_ref[b, h : h + 1, :] for b, ref in enumerate((own_o, mate_o, line_o, side_o)))
        turn(h, out, att_buf)
    att_copy = pltpu.make_async_copy(att_buf, att_ref, sems.at[0])
    gq_copy = pltpu.make_async_copy(buf, gq_ref, sems.at[1])
    att_copy.start()

    @pl.when(lax.axis_index("ctx") >= 0)
    def _():
        backward_queries(
            g_ref, kv_ref, e_ref, scale_ref.at[OWN], delta_ref, lambda h, v: turn(h, (gq_in[h] + v) * factor, buf),
            kt_ref, p_ref, ds_ref, dp_ref,
        )

    gq_copy.start()

    @pl.when(lax.axis_index("ctx") >= 0)
    def _():
        backward_keys(q_ref, g_ref, p_ref, ds_ref, part_ref)

    att_copy.wait()
    gq_copy.wait()


def line_add_kernel(line_ref, mate_ref, out_ref):
    out_ref[...] = (line_ref[...] + mate_ref[...].astype(jnp.float32)).astype(jnp.bfloat16)


def line_sum_kernel(own_ref, line_ref, out_ref):
    out_ref[...] = own_ref[...] + line_ref[...].astype(jnp.float32)


def side_sum_kernel(sum_ref, near_ref, far_ref, k_ref, v_ref):
    here, count = lax.axis_index("ctx"), lax.axis_size("ctx")
    dim = k_ref.shape[1]
    even = lax.rem(here, 2) == 0
    side = jnp.where(even, near_ref[...].astype(jnp.float32), far_ref[...].astype(jnp.float32))
    total = sum_ref[...] + jnp.where(even | (here + 3 < count), side, 0.0)
    k_ref[...] = total[:, :dim].astype(jnp.bfloat16)
    v_ref[...] = total[:, dim:].astype(jnp.bfloat16)


def call(name, kernel, args, outs, scratch, flops, far_in=(), far_out=(), aliases=None):
    near, far = pl.BlockSpec(memory_space=pltpu.VMEM), pl.BlockSpec(memory_space=pltpu.HBM)
    args = [pltpu.with_memory_space_constraint(a, pltpu.HBM) if i in far_in else a for i, a in enumerate(args)]
    return pl.pallas_call(
        kernel,
        name=name,
        out_shape=outs,
        in_specs=[far if i in far_in else near for i in range(len(args))],
        out_specs=[far if i in far_out else near for i in range(len(outs))],
        scratch_shapes=scratch,
        input_output_aliases=aliases or {},
        cost_estimate=pl.CostEstimate(flops=flops, bytes_accessed=0, transcendentals=0),
        compiler_params=pltpu.CompilerParams(vmem_limit_bytes=16 << 20),
    )(*args)


def three_back(count):
    to = {i: i - 3 for i in range(4, count, 2)}
    to.update({i: i + 3 for i in range(3, count - 3, 2)})
    to.update({0: 2, 1: 0, 2: 4, count - 3: count - 1, count - 1: count - 3})
    return list(to.items())


def body(queries, key_vectors, value_vectors, doc_ids, grad_out):
    rows, dim = key_vectors.shape
    heads = queries.shape[1] // dim
    count = lax.axis_size("ctx")
    to_mate = [(i, i ^ 1) for i in range(count)]
    to_line = [(i, (i + 2) % count) for i in range(count)]
    to_side = [(i, (i + 1 + 2 * (i % 2)) % count) for i in range(count)]
    flip = lambda pairs: [(b, a) for a, b in pairs]
    f32, bf16 = jnp.float32, jnp.bfloat16
    shape = jax.ShapeDtypeStruct
    e_shape, stat_shape, out_shape = shape((heads, rows, rows), bf16), shape((3 * heads, rows), f32), shape((heads, dim, rows), f32)
    pair, pair_sent = shape((rows, 2 * dim), f32), shape((rows, 2 * dim), bf16)
    wide = shape(queries.shape, bf16)
    buffer = lambda like: pltpu.VMEM(like.shape, like.dtype)
    flat = pltpu.VMEM((dim, rows), bf16)
    ahead = [pltpu.VMEM((heads, rows, rows), f32), flat]
    back = [flat, buffer(e_shape), buffer(e_shape)]
    work = heads * rows

    docs = doc_ids.reshape(-1, LANES)
    own = call(
        "pack", pack_kernel, (key_vectors, value_vectors), (pair_sent,), [pltpu.SemaphoreType.DMA((2,))], 0, (0, 1)
    )[0]
    own = call("settle", settle_kernel, (own,), (pair_sent,), [], 1 << 33, (), (), {0: 0})[0]
    line = lax.ppermute(own, "ctx", to_line)
    q, g = queries, grad_out
    own_e, own_stat, own_o, bias, gt, dp, seen = call(
        "own_forward", own_kernel, (docs, q, g, own),
        (e_shape, stat_shape, out_shape, shape((3, rows, rows), f32), shape((heads, dim, rows), bf16), shape((heads, rows, rows), f32),
         shape((8, LANES), jnp.int32)),
        [pltpu.VMEM((rows, rows), f32), *ahead], work,
    )
    line, own_stat = lax.optimization_barrier((line, own_stat))
    side = lax.ppermute(own, "ctx", to_side)
    mate = lax.ppermute(line, "ctx", to_mate)

    def first(name, role, kv):
        return call(
            name, lambda *refs: next_kernel(role, *refs), (seen, q, kv, bias, gt), (e_shape, stat_shape, out_shape), ahead, work
        )

    line_e, line_stat, line_o = first("line_forward", LINE, line)
    side_e, side_stat, side_o = first("side_forward", SIDE, side)
    mate_o, mate_part, early_part, gq, scales, delta = call(
        "rest_forward", rest_kernel,
        (seen, q, g, mate, side, bias, gt, own_stat, line_stat, side_stat, side_e),
        (out_shape, pair_sent, pair_sent, out_shape, shape((4, heads, rows), f32), shape((heads, rows), f32)),
        [*ahead, buffer(e_shape), buffer(stat_shape), *back],
        work,
    )
    mate_back = lax.ppermute(mate_part, "ctx", to_mate)
    line_part, gq = call(
        "line_backward", line_kernel, (seen, q, g, line, line_e, scales, delta, gq), (pair, out_shape), back, work
    )
    line_part = call("line_add", line_add_kernel, (line_part, mate_back), (pair_sent,), [], 0)[0]
    line_part, gq = lax.optimization_barrier((line_part, gq))
    side_part, gq = call(
        "side_backward", side_kernel, (seen, q, g, side, side_e, scales, delta, gq, early_part), (pair_sent, out_shape), back, work
    )
    side_far = lax.ppermute(side_part, "ctx", three_back(count))
    side_near = lax.ppermute(side_part, "ctx", to_mate)
    line_back = lax.ppermute(line_part, "ctx", flip(to_line))
    own_part, grad_query, attended = call(
        "own_backward", last_kernel, (q, g, own, own_e, scales, delta, gq, dp, own_o, mate_o, line_o, side_o), (pair, wide, wide),
        [*back, buffer(wide), buffer(wide), pltpu.SemaphoreType.DMA((2,))], work, (), (1, 2),
    )
    total = call("line_sum", line_sum_kernel, (own_part, line_back), (pair,), [], work)[0]
    narrow = shape((rows, dim), bf16)
    grad_key, grad_value = call("side_sum", side_sum_kernel, (total, side_near, side_far), (narrow, narrow), [], 0)
    return attended, grad_query, grad_key, grad_value


def solution(mesh):
    return jax.shard_map(
        body,
        mesh=mesh,
        in_specs=(P("ctx", "head"), P("ctx", "head"), P("ctx", "head"), P(), P("ctx", "head")),
        out_specs=(P("ctx", "head"), P("ctx", "head"), P("ctx", "head"), P("ctx", "head")),
        check_vma=False,
    )
```

```python
import jax
import jax.numpy as jnp
from jax import lax
from jax.experimental import pallas as pl
from jax.experimental.pallas import tpu as pltpu
from jax.sharding import PartitionSpec as P

LANES = 128
LOG2_E = 1.4426950408889634
MASKED = -1e30

OWN, MATE, LINE, SIDE = range(4)


def nt(a, b):
    return lax.dot_general(a, b, (((1,), (1,)), ((), ())), preferred_element_type=jnp.float32)


def nn(a, b):
    return lax.dot_general(a, b, (((1,), (0,)), ((), ())), preferred_element_type=jnp.float32)


def place(role, rows):
    here, count = lax.axis_index("ctx"), lax.axis_size("ctx")
    odd = lax.rem(here, 2)
    block = here - (0, 1 + 2 * odd, 2, 3 - 2 * odd)[role]
    steps = rows // LANES
    return here * steps, lax.rem(block + count, count) * steps, block >= 0


def find_seen(role, doc_ref, rows):
    mine, at, valid = place(role, rows)
    steps = rows // LANES
    first = jnp.min(doc_ref[pl.ds(mine, 1), :].astype(jnp.float32))
    last = jnp.max(doc_ref[pl.ds(at + steps - 1, 1), :].astype(jnp.float32))
    middle = jnp.max(doc_ref[pl.ds(at + steps // 2 - 1, 1), :].astype(jnp.float32))
    level = (last == first).astype(jnp.int32) + (middle == first).astype(jnp.int32)
    return jnp.where(valid, level, 0)


def seen_level(role, seen_ref):
    return seen_ref[role : role + 1, :][0, 0]


def is_seen(role, seen_ref):
    return seen_ref[role : role + 1, :][0, 0] > 0


def mask_bias(role, doc_ref, bias):
    rows = bias.shape[0]
    steps = rows // LANES
    mine, at, valid = place(role, rows)
    own_doc = jnp.concatenate([doc_ref[pl.ds(mine + i, 1), :] for i in range(steps)], axis=1)
    for i in range(steps):
        row = jnp.where(valid, doc_ref[pl.ds(at + i, 1), :], -1)
        column = jnp.transpose(jnp.broadcast_to(row, (LANES, LANES)).astype(jnp.float32)).astype(jnp.int32)
        same = jnp.concatenate([column] * steps, axis=1) == own_doc
        if role == OWN:
            key_at = lax.broadcasted_iota(jnp.int32, (LANES, rows), 0) + i * LANES
            same = same & (key_at <= lax.broadcasted_iota(jnp.int32, (LANES, rows), 1))
        bias[i * LANES : (i + 1) * LANES, :] = jnp.where(same, 0.0, MASKED)


def forward(q_ref, kv_ref, bias, gt_ref, e_ref, stat_ref, out_ref, s_ref, vt_ref, start=0):
    dim = kv_ref.shape[1] // 2
    heads = q_ref.shape[1] // dim
    factor = dim**-0.5 * LOG2_E
    keys = slice(start, kv_ref.shape[0])
    vt_ref[:, keys] = jnp.transpose(kv_ref[keys, dim:])
    for h in range(heads):
        s_ref[h, keys, :] = nt(kv_ref[keys, :dim], q_ref[:, h * dim : (h + 1) * dim])
    for h in range(heads):
        s = s_ref[h, keys, :] * factor + bias[keys, :]
        top = jnp.max(s, axis=0, keepdims=True)
        e = jnp.exp2(s - top)
        e_ref[h, keys, :] = e.astype(jnp.bfloat16)
        stat_ref[h : h + 1, :] = top
        stat_ref[heads + h : heads + h + 1, :] = jnp.sum(e, axis=0, keepdims=True)
    for h in range(heads):
        out = nn(vt_ref[:, keys], e_ref[h, keys, :])
        out_ref[h] = out
        stat_ref[2 * heads + h : 2 * heads + h + 1, :] = jnp.sum(out * gt_ref[h].astype(jnp.float32), axis=0, keepdims=True)


def forward_unseen(stat_ref, out_ref):
    heads = out_ref.shape[0]
    stat_ref[:heads, :] = jnp.full((heads, stat_ref.shape[1]), MASKED, jnp.float32)
    stat_ref[heads:, :] = jnp.zeros((2 * heads, stat_ref.shape[1]), jnp.float32)
    out_ref[...] = jnp.zeros(out_ref.shape, out_ref.dtype)


def backward_queries(g_ref, kv_ref, e_ref, scale_ref, delta_ref, gq_out, kt_ref, p_ref, ds_ref, dp=None, start=0):
    dim = kv_ref.shape[1] // 2
    heads = g_ref.shape[1] // dim
    keys = slice(start, kv_ref.shape[0])
    kt_ref[:, keys] = jnp.transpose(kv_ref[keys, :dim])
    for h in range(heads):
        probs = e_ref[h, keys, :] * scale_ref[h : h + 1, :].astype(jnp.bfloat16)
        p_ref[h, keys, :] = probs
        grad_p = nt(kv_ref[keys, dim:], g_ref[:, h * dim : (h + 1) * dim]) if dp is None else dp[h]
        ds_ref[h, keys, :] = probs * (grad_p - delta_ref[h : h + 1, :]).astype(jnp.bfloat16)
    for h in range(heads):
        gq_out(h, nn(kt_ref[:, keys], ds_ref[h, keys, :]))


def backward_keys(q_ref, g_ref, p_ref, ds_ref, part_ref, start=0):
    rows, dim = part_ref.shape[0], part_ref.shape[1] // 2
    keys = slice(start, rows)
    cols = [slice(h * dim, (h + 1) * dim) for h in range(q_ref.shape[1] // dim)]
    if start:
        part_ref[:start, :] = jnp.zeros((start, 2 * dim), part_ref.dtype)
    grad_v = sum(nn(p_ref[h, keys, :], g_ref[:, c]) for h, c in enumerate(cols))
    part_ref[keys, dim:] = grad_v.astype(part_ref.dtype)
    grad_k = sum(nn(ds_ref[h, keys, :], q_ref[:, c]) for h, c in enumerate(cols))
    part_ref[keys, :dim] = (grad_k * dim**-0.5).astype(part_ref.dtype)


def backward_unseen(part_ref, gq_in, gq_ref):
    part_ref[...] = jnp.zeros(part_ref.shape, part_ref.dtype)
    gq_ref[...] = jnp.zeros(gq_ref.shape, gq_ref.dtype) if gq_in is None else gq_in[...]


def pack_kernel(k_ref, v_ref, kv_ref, sems):
    dim = k_ref.shape[1]
    copies = [
        pltpu.make_async_copy(ref, kv_ref.at[:, i * dim : (i + 1) * dim], sems.at[i]) for i, ref in enumerate((k_ref, v_ref))
    ]
    for copy in copies:
        copy.start()
    for copy in copies:
        copy.wait()


def settle_kernel(in_ref, out_ref):
    out_ref[:16, :] = in_ref[:16, :]


def own_kernel(doc_ref, q_ref, g_ref, kv_ref, e_ref, stat_ref, out_ref, bias_ref, gt_ref, dp_ref, seen_ref, bias, s_ref, vt_ref):
    dim = kv_ref.shape[1] // 2
    heads = q_ref.shape[1] // dim
    mask_bias(OWN, doc_ref, bias)
    for h in range(heads):
        gt_ref[h] = jnp.transpose(g_ref[:, h * dim : (h + 1) * dim])
    forward(q_ref, kv_ref, bias, gt_ref, e_ref, stat_ref, out_ref, s_ref, vt_ref)
    for role in (MATE, LINE, SIDE):
        mask_bias(role, doc_ref, bias_ref.at[role - 1])
        seen = find_seen(role, doc_ref, kv_ref.shape[0])
        seen_ref[role : role + 1, :] = jnp.full((1, LANES), seen, jnp.int32)
    for h in range(heads):
        dp_ref[h] = nt(kv_ref[:, dim:], g_ref[:, h * dim : (h + 1) * dim])


def next_kernel(role, seen_ref, q_ref, kv_ref, bias_ref, gt_ref, e_ref, stat_ref, out_ref, s_ref, vt_ref):
    level = seen_level(role, seen_ref)
    for some, start in ((2, 0), (1, kv_ref.shape[0] // 2)):

        @pl.when(level == some)
        def _():
            forward(q_ref, kv_ref, bias_ref.at[role - 1], gt_ref, e_ref, stat_ref, out_ref, s_ref, vt_ref, start)

    @pl.when(level == 0)
    def _():
        forward_unseen(stat_ref, out_ref)


def next_backward(level, q_ref, g_ref, kv_ref, e_ref, scale_ref, delta_ref, gq_in, part_ref, gq_ref, kt_ref, p_ref, ds_ref):
    def put(h, value):
        gq_ref[h] = value if gq_in is None else gq_in[h] + value

    for some, start in ((2, 0), (1, kv_ref.shape[0] // 2)):

        @pl.when(level == some)
        def _():
            backward_queries(g_ref, kv_ref, e_ref, scale_ref, delta_ref, put, kt_ref, p_ref, ds_ref, None, start)
            backward_keys(q_ref, g_ref, p_ref, ds_ref, part_ref, start)

    @pl.when(level == 0)
    def _():
        backward_unseen(part_ref, gq_in, gq_ref)


def rest_kernel(
    seen_ref, q_ref, g_ref, mate_ref, side_ref, bias_ref, gt_ref, own_stat, line_stat, side_stat, side_e,
    mate_o, mate_part, side_part, gq_part, scale_ref, delta_ref,
    s_ref, vt_ref, mate_e, mate_stat, kt_ref, p_ref, ds_ref,
):
    dim = mate_ref.shape[1] // 2
    heads = q_ref.shape[1] // dim
    next_kernel(MATE, seen_ref, q_ref, mate_ref, bias_ref, gt_ref, mate_e, mate_stat, mate_o, s_ref, vt_ref)
    stats = (own_stat, mate_stat, line_stat, side_stat)
    tops = [ref[:heads, :] for ref in stats]
    top = jnp.maximum(jnp.maximum(tops[0], tops[1]), jnp.maximum(tops[2], tops[3]))
    parts = [jnp.exp2(t - top) for t in tops]
    inverse = 1.0 / sum(p * ref[heads : 2 * heads, :] for p, ref in zip(parts, stats))
    for b in range(4):
        scale_ref[b] = parts[b] * inverse
    delta_ref[...] = sum(p * ref[2 * heads :, :] for p, ref in zip(parts, stats)) * inverse
    rows = mate_ref.shape[0]
    seen = is_seen(MATE, seen_ref)

    @pl.when(seen)
    def _():
        next_backward(
            seen_level(MATE, seen_ref), q_ref, g_ref, mate_ref, mate_e, scale_ref.at[MATE], delta_ref, None, mate_part, gq_part, kt_ref, p_ref, ds_ref
        )

    @pl.when(jnp.logical_not(seen))
    def _():
        mate_part[...] = jnp.zeros(mate_part.shape, mate_part.dtype)
        next_backward(
            seen_level(SIDE, seen_ref), q_ref, g_ref, side_ref, side_e, scale_ref.at[SIDE], delta_ref, None,
            side_part, gq_part, kt_ref, p_ref, ds_ref,
        )


def line_kernel(seen_ref, q_ref, g_ref, kv_ref, e_ref, scale_ref, delta_ref, gq_in, part_ref, gq_ref, kt_ref, p_ref, ds_ref):
    next_backward(
        seen_level(LINE, seen_ref), q_ref, g_ref, kv_ref, e_ref, scale_ref.at[LINE], delta_ref, gq_in,
        part_ref, gq_ref, kt_ref, p_ref, ds_ref,
    )


def side_kernel(
    seen_ref, q_ref, g_ref, kv_ref, e_ref, scale_ref, delta_ref, gq_in, early_part, line_part,
    part_ref, near_ref, gq_ref, kt_ref, p_ref, ds_ref,
):
    late = is_seen(MATE, seen_ref)

    @pl.when(late)
    def _():
        next_backward(
            seen_level(SIDE, seen_ref), q_ref, g_ref, kv_ref, e_ref, scale_ref.at[SIDE], delta_ref, gq_in,
            part_ref, gq_ref, kt_ref, p_ref, ds_ref,
        )

    @pl.when(jnp.logical_not(late))
    def _():
        part_ref[...] = early_part[...]
        gq_ref[...] = gq_in[...]

    joint = is_joint(lax.axis_index("ctx") // 2, lax.axis_size("ctx") // 2)
    near_ref[...] = jnp.where(joint, line_part[...], part_ref[...])


def turn(h, value, buf):
    buf[:, h * value.shape[0] : (h + 1) * value.shape[0]] = jnp.transpose(value.astype(jnp.bfloat16))


def last_kernel(
    q_ref, g_ref, kv_ref, e_ref, scale_ref, delta_ref, gq_in, dp_ref, own_o, mate_o, line_o, side_o, part_ref, gq_ref, att_ref,
    kt_ref, p_ref, ds_ref, buf, att_buf, sems,
):
    factor = (kv_ref.shape[1] // 2) ** -0.5
    for h in range(own_o.shape[0]):
        out = sum(ref[h] * scale_ref[b, h : h + 1, :] for b, ref in enumerate((own_o, mate_o, line_o, side_o)))
        turn(h, out, att_buf)
    att_copy = pltpu.make_async_copy(att_buf, att_ref, sems.at[0])
    gq_copy = pltpu.make_async_copy(buf, gq_ref, sems.at[1])
    att_copy.start()

    @pl.when(lax.axis_index("ctx") >= 0)
    def _():
        backward_queries(
            g_ref, kv_ref, e_ref, scale_ref.at[OWN], delta_ref, lambda h, v: turn(h, (gq_in[h] + v) * factor, buf),
            kt_ref, p_ref, ds_ref, dp_ref,
        )

    gq_copy.start()

    @pl.when(lax.axis_index("ctx") >= 0)
    def _():
        backward_keys(q_ref, g_ref, p_ref, ds_ref, part_ref)

    att_copy.wait()
    gq_copy.wait()


def line_add_kernel(line_ref, mate_ref, out_ref):
    out_ref[...] = (line_ref[...] + mate_ref[...].astype(jnp.float32)).astype(jnp.bfloat16)


def line_sum_kernel(own_ref, line_ref, out_ref):
    chip, chips = lax.axis_index("ctx") // 2, lax.axis_size("ctx") // 2
    in_ring = (chip < chips - 1) & (chip != chips - SECOND - 1)
    out_ref[...] = own_ref[...] + jnp.where(in_ring, line_ref[...].astype(jnp.float32), 0.0)


def near_sum_kernel(sum_ref, near_ref, out_ref):
    here, count = lax.axis_index("ctx"), lax.axis_size("ctx")
    chip = here // 2
    even, joint = lax.rem(here, 2) == 0, is_joint(chip, count // 2)
    taken = (chip == count // 2 - SECOND - 1) | (jnp.logical_not(joint) & even)
    out_ref[...] = sum_ref[...] + jnp.where(taken, near_ref[...].astype(jnp.float32), 0.0)


def far_sum_kernel(sum_ref, far_ref, k_ref, v_ref):
    here, count = lax.axis_index("ctx"), lax.axis_size("ctx")
    dim, even = k_ref.shape[1], lax.rem(here, 2) == 0
    taken = (even & is_joint(here // 2, count // 2)) | (jnp.logical_not(even) & (here + 3 < count))
    total = sum_ref[...] + jnp.where(taken, far_ref[...].astype(jnp.float32), 0.0)
    k_ref[...] = total[:, :dim].astype(jnp.bfloat16)
    v_ref[...] = total[:, dim:].astype(jnp.bfloat16)


def call(name, kernel, args, outs, scratch, flops, far_in=(), far_out=(), aliases=None):
    near, far = pl.BlockSpec(memory_space=pltpu.VMEM), pl.BlockSpec(memory_space=pltpu.HBM)
    args = [pltpu.with_memory_space_constraint(a, pltpu.HBM) if i in far_in else a for i, a in enumerate(args)]
    return pl.pallas_call(
        kernel,
        name=name,
        out_shape=outs,
        in_specs=[far if i in far_in else near for i in range(len(args))],
        out_specs=[far if i in far_out else near for i in range(len(outs))],
        scratch_shapes=scratch,
        input_output_aliases=aliases or {},
        cost_estimate=pl.CostEstimate(flops=flops, bytes_accessed=0, transcendentals=0),
        compiler_params=pltpu.CompilerParams(vmem_limit_bytes=16 << 20),
    )(*args)


SECOND = 3


def line_rings(count):
    to = {i: i - 2 for i in range(count)}
    first = count - 2 * SECOND
    to.update({core: first - 2 + core for core in (0, 1)})
    to.update({first + core: count - 2 + core for core in (0, 1)})
    return list(to.items())


def is_joint(chip, chips):
    return (chip == chips - SECOND - 1) | (chip == chips - SECOND)


def near_swaps(count):
    to = {i: i ^ 1 for i in range(count)}
    first = count - 2 * SECOND
    for i in (first - 2, first - 1):
        to[i], to[i + 2] = i + 2, i
    return list(to.items())


def three_back(count):
    to = {i: i - 3 for i in range(4, count, 2)}
    to.update({i: i + 3 for i in range(3, count - 3, 2)})
    to.update({0: 2, 1: 0, 2: 4, count - 3: count - 1, count - 1: count - 3})
    i = count - 2 * SECOND - 1
    to.update({i: i - 1, i + 2: i + 1, i - 4: i + 3, i - 2: i + 5})
    return list(to.items())


def body(queries, key_vectors, value_vectors, doc_ids, grad_out):
    rows, dim = key_vectors.shape
    heads = queries.shape[1] // dim
    count = lax.axis_size("ctx")
    to_mate = [(i, i ^ 1) for i in range(count)]
    to_line = [(i, (i + 2) % count) for i in range(count)]
    to_side = [(i, (i + 1 + 2 * (i % 2)) % count) for i in range(count)]
    f32, bf16 = jnp.float32, jnp.bfloat16
    shape = jax.ShapeDtypeStruct
    e_shape, stat_shape, out_shape = shape((heads, rows, rows), bf16), shape((3 * heads, rows), f32), shape((heads, dim, rows), f32)
    pair, pair_sent = shape((rows, 2 * dim), f32), shape((rows, 2 * dim), bf16)
    wide = shape(queries.shape, bf16)
    buffer = lambda like: pltpu.VMEM(like.shape, like.dtype)
    flat = pltpu.VMEM((dim, rows), bf16)
    ahead = [pltpu.VMEM((heads, rows, rows), f32), flat]
    back = [flat, buffer(e_shape), buffer(e_shape)]
    work = heads * rows

    docs = doc_ids.reshape(-1, LANES)
    own = call(
        "pack", pack_kernel, (key_vectors, value_vectors), (pair_sent,), [pltpu.SemaphoreType.DMA((2,))], 0, (0, 1)
    )[0]
    own = call("settle", settle_kernel, (own,), (pair_sent,), [], 1 << 33, (), (), {0: 0})[0]
    line = lax.ppermute(own, "ctx", to_line)
    q, g = queries, grad_out
    own_e, own_stat, own_o, bias, gt, dp, seen = call(
        "own_forward", own_kernel, (docs, q, g, own),
        (e_shape, stat_shape, out_shape, shape((3, rows, rows), f32), shape((heads, dim, rows), bf16), shape((heads, rows, rows), f32),
         shape((8, LANES), jnp.int32)),
        [pltpu.VMEM((rows, rows), f32), *ahead], work,
    )
    line, own_stat = lax.optimization_barrier((line, own_stat))
    side = lax.ppermute(own, "ctx", to_side)
    mate = lax.ppermute(line, "ctx", to_mate)

    def first(name, role, kv):
        return call(
            name, lambda *refs: next_kernel(role, *refs), (seen, q, kv, bias, gt), (e_shape, stat_shape, out_shape), ahead, work
        )

    line_e, line_stat, line_o = first("line_forward", LINE, line)
    side_e, side_stat, side_o = first("side_forward", SIDE, side)
    mate_o, mate_part, early_part, gq, scales, delta = call(
        "rest_forward", rest_kernel,
        (seen, q, g, mate, side, bias, gt, own_stat, line_stat, side_stat, side_e),
        (out_shape, pair_sent, pair_sent, out_shape, shape((4, heads, rows), f32), shape((heads, rows), f32)),
        [*ahead, buffer(e_shape), buffer(stat_shape), *back],
        work,
    )
    mate_back = lax.ppermute(mate_part, "ctx", to_mate)
    line_part, gq = call(
        "line_backward", line_kernel, (seen, q, g, line, line_e, scales, delta, gq), (pair, out_shape), back, work
    )
    line_part = call("line_add", line_add_kernel, (line_part, mate_back), (pair_sent,), [], 0)[0]
    line_part, gq = lax.optimization_barrier((line_part, gq))
    side_part, near_part, gq = call(
        "side_backward", side_kernel, (seen, q, g, side, side_e, scales, delta, gq, early_part, line_part),
        (pair_sent, pair_sent, out_shape), back, work,
    )
    side_far = lax.ppermute(side_part, "ctx", three_back(count))
    side_near = lax.ppermute(near_part, "ctx", near_swaps(count))
    line_back = lax.ppermute(line_part, "ctx", line_rings(count))
    own_part, grad_query, attended = call(
        "own_backward", last_kernel, (q, g, own, own_e, scales, delta, gq, dp, own_o, mate_o, line_o, side_o), (pair, wide, wide),
        [*back, buffer(wide), buffer(wide), pltpu.SemaphoreType.DMA((2,))], work, (), (1, 2),
    )
    total = call("line_sum", line_sum_kernel, (own_part, line_back), (pair,), [], work)[0]
    narrow = shape((rows, dim), bf16)
    total = call("near_sum", near_sum_kernel, (total, side_near), (pair,), [], work)[0]
    grad_key, grad_value = call("far_sum", far_sum_kernel, (total, side_far), (narrow, narrow), [], 0)
    return attended, grad_query, grad_key, grad_value


def solution(mesh):
    return jax.shard_map(
        body,
        mesh=mesh,
        in_specs=(P("ctx", "head"), P("ctx", "head"), P("ctx", "head"), P(), P("ctx", "head")),
        out_specs=(P("ctx", "head"), P("ctx", "head"), P("ctx", "head"), P("ctx", "head")),
        check_vma=False,
    )
```

```python
import jax
import jax.numpy as jnp
from jax import lax
from jax.experimental import pallas as pl
from jax.experimental.pallas import tpu as pltpu
from jax.sharding import PartitionSpec as P

LANES = 128
LOG2_E = 1.4426950408889634
MASKED = -1e30

OWN, MATE, LINE, SIDE = range(4)


def nt(a, b):
    return lax.dot_general(a, b, (((1,), (1,)), ((), ())), preferred_element_type=jnp.float32)


def nn(a, b):
    return lax.dot_general(a, b, (((1,), (0,)), ((), ())), preferred_element_type=jnp.float32)


def place(role, rows):
    here, count = lax.axis_index("ctx"), lax.axis_size("ctx")
    odd = lax.rem(here, 2)
    block = here - (0, 1 + 2 * odd, 2, 3 - 2 * odd)[role]
    steps = rows // LANES
    return here * steps, lax.rem(block + count, count) * steps, block >= 0


def find_seen(role, doc_ref, rows):
    mine, at, valid = place(role, rows)
    steps = rows // LANES
    first = jnp.min(doc_ref[pl.ds(mine, 1), :].astype(jnp.float32))
    last = jnp.max(doc_ref[pl.ds(at + steps - 1, 1), :].astype(jnp.float32))
    middle = jnp.max(doc_ref[pl.ds(at + steps // 2 - 1, 1), :].astype(jnp.float32))
    level = (last == first).astype(jnp.int32) + (middle == first).astype(jnp.int32)
    return jnp.where(valid, level, 0)


def seen_level(role, seen_ref):
    return seen_ref[role : role + 1, :][0, 0]


def is_seen(role, seen_ref):
    return seen_ref[role : role + 1, :][0, 0] > 0


def mask_bias(role, doc_ref, bias):
    rows = bias.shape[0]
    steps = rows // LANES
    mine, at, valid = place(role, rows)
    own_doc = jnp.concatenate([doc_ref[pl.ds(mine + i, 1), :] for i in range(steps)], axis=1)
    for i in range(steps):
        row = jnp.where(valid, doc_ref[pl.ds(at + i, 1), :], -1)
        column = jnp.transpose(jnp.broadcast_to(row, (LANES, LANES)).astype(jnp.float32)).astype(jnp.int32)
        same = jnp.concatenate([column] * steps, axis=1) == own_doc
        if role == OWN:
            key_at = lax.broadcasted_iota(jnp.int32, (LANES, rows), 0) + i * LANES
            same = same & (key_at <= lax.broadcasted_iota(jnp.int32, (LANES, rows), 1))
        bias[i * LANES : (i + 1) * LANES, :] = jnp.where(same, 0.0, MASKED)


def forward(q_ref, kv_ref, bias, gt_ref, e_ref, stat_ref, out_ref, s_ref, vt_ref, start=0):
    dim = kv_ref.shape[1] // 2
    heads = q_ref.shape[1] // dim
    factor = dim**-0.5 * LOG2_E
    keys = slice(start, kv_ref.shape[0])
    vt_ref[:, keys] = jnp.transpose(kv_ref[keys, dim:])
    for h in range(heads):
        s_ref[h, keys, :] = nt(kv_ref[keys, :dim], q_ref[:, h * dim : (h + 1) * dim])
    for h in range(heads):
        s = s_ref[h, keys, :] * factor + bias[keys, :]
        top = jnp.max(s, axis=0, keepdims=True)
        e = jnp.exp2(s - top)
        e_ref[h, keys, :] = e.astype(jnp.bfloat16)
        stat_ref[h : h + 1, :] = top
        stat_ref[heads + h : heads + h + 1, :] = jnp.sum(e, axis=0, keepdims=True)
    for h in range(heads):
        out = nn(vt_ref[:, keys], e_ref[h, keys, :])
        out_ref[h] = out
        stat_ref[2 * heads + h : 2 * heads + h + 1, :] = jnp.sum(out * gt_ref[h].astype(jnp.float32), axis=0, keepdims=True)


def forward_unseen(stat_ref):
    heads = stat_ref.shape[0] // 3
    stat_ref[:heads, :] = jnp.full((heads, stat_ref.shape[1]), MASKED, jnp.float32)
    stat_ref[heads:, :] = jnp.zeros((2 * heads, stat_ref.shape[1]), jnp.float32)


def backward_queries(g_ref, kv_ref, e_ref, scale_ref, delta_ref, gq_out, kt_ref, p_ref, ds_ref, dp=None, start=0):
    dim = kv_ref.shape[1] // 2
    heads = g_ref.shape[1] // dim
    keys = slice(start, kv_ref.shape[0])
    kt_ref[:, keys] = jnp.transpose(kv_ref[keys, :dim])
    for h in range(heads):
        probs = e_ref[h, keys, :] * scale_ref[h : h + 1, :].astype(jnp.bfloat16)
        p_ref[h, keys, :] = probs
        grad_p = nt(kv_ref[keys, dim:], g_ref[:, h * dim : (h + 1) * dim]) if dp is None else dp[h]
        ds_ref[h, keys, :] = probs * (grad_p - delta_ref[h : h + 1, :]).astype(jnp.bfloat16)
    for h in range(heads):
        gq_out(h, nn(kt_ref[:, keys], ds_ref[h, keys, :]))


def backward_keys(q_ref, g_ref, p_ref, ds_ref, part_ref, start=0):
    rows, dim = part_ref.shape[0], part_ref.shape[1] // 2
    keys = slice(start, rows)
    cols = [slice(h * dim, (h + 1) * dim) for h in range(q_ref.shape[1] // dim)]
    if start:
        part_ref[:start, :] = jnp.zeros((start, 2 * dim), part_ref.dtype)
    grad_v = sum(nn(p_ref[h, keys, :], g_ref[:, c]) for h, c in enumerate(cols))
    part_ref[keys, dim:] = grad_v.astype(part_ref.dtype)
    grad_k = sum(nn(ds_ref[h, keys, :], q_ref[:, c]) for h, c in enumerate(cols))
    part_ref[keys, :dim] = (grad_k * dim**-0.5).astype(part_ref.dtype)


def backward_unseen(part_ref, gq_in, gq_ref):
    part_ref[...] = jnp.zeros(part_ref.shape, part_ref.dtype)
    gq_ref[...] = jnp.zeros(gq_ref.shape, gq_ref.dtype) if gq_in is None else gq_in[...]


def pack_kernel(k_ref, v_ref, kv_ref, sems):
    dim = k_ref.shape[1]
    copies = [
        pltpu.make_async_copy(ref, kv_ref.at[:, i * dim : (i + 1) * dim], sems.at[i]) for i, ref in enumerate((k_ref, v_ref))
    ]
    for copy in copies:
        copy.start()
    for copy in copies:
        copy.wait()


def own_kernel(doc_ref, q_ref, g_ref, kv_ref, e_ref, stat_ref, out_ref, bias_ref, gt_ref, dp_ref, seen_ref, bias, s_ref, vt_ref):
    dim = kv_ref.shape[1] // 2
    heads = q_ref.shape[1] // dim
    mask_bias(OWN, doc_ref, bias)
    for h in range(heads):
        gt_ref[h] = jnp.transpose(g_ref[:, h * dim : (h + 1) * dim])
    forward(q_ref, kv_ref, bias, gt_ref, e_ref, stat_ref, out_ref, s_ref, vt_ref)
    for role in (MATE, LINE, SIDE):
        mask_bias(role, doc_ref, bias_ref.at[role - 1])
        seen = find_seen(role, doc_ref, kv_ref.shape[0])
        seen_ref[role : role + 1, :] = jnp.full((1, LANES), seen, jnp.int32)
    for h in range(heads):
        dp_ref[h] = nt(kv_ref[:, dim:], g_ref[:, h * dim : (h + 1) * dim])


def next_kernel(role, seen_ref, q_ref, kv_ref, bias_ref, gt_ref, e_ref, stat_ref, out_ref, s_ref, vt_ref):
    level = seen_level(role, seen_ref)
    for some, start in ((2, 0), (1, kv_ref.shape[0] // 2)):

        @pl.when(level == some)
        def _():
            forward(q_ref, kv_ref, bias_ref.at[role - 1], gt_ref, e_ref, stat_ref, out_ref, s_ref, vt_ref, start)

    @pl.when(level == 0)
    def _():
        forward_unseen(stat_ref)


def next_backward(level, q_ref, g_ref, kv_ref, e_ref, scale_ref, delta_ref, gq_in, part_ref, gq_ref, kt_ref, p_ref, ds_ref):
    def put(h, value):
        gq_ref[h] = value if gq_in is None else gq_in[h] + value

    for some, start in ((2, 0), (1, kv_ref.shape[0] // 2)):

        @pl.when(level == some)
        def _():
            backward_queries(g_ref, kv_ref, e_ref, scale_ref, delta_ref, put, kt_ref, p_ref, ds_ref, None, start)
            backward_keys(q_ref, g_ref, p_ref, ds_ref, part_ref, start)

    @pl.when(level == 0)
    def _():
        backward_unseen(part_ref, gq_in, gq_ref)


def rest_kernel(
    seen_ref, q_ref, g_ref, mate_ref, side_ref, bias_ref, gt_ref, own_stat, line_stat, side_stat, side_e,
    mate_o, mate_part, side_part, gq_part, scale_ref, delta_ref,
    s_ref, vt_ref, mate_e, mate_stat, kt_ref, p_ref, ds_ref,
):
    dim = mate_ref.shape[1] // 2
    heads = q_ref.shape[1] // dim
    next_kernel(MATE, seen_ref, q_ref, mate_ref, bias_ref, gt_ref, mate_e, mate_stat, mate_o, s_ref, vt_ref)
    stats = (own_stat, mate_stat, line_stat, side_stat)
    tops = [ref[:heads, :] for ref in stats]
    top = jnp.maximum(jnp.maximum(tops[0], tops[1]), jnp.maximum(tops[2], tops[3]))
    parts = [jnp.exp2(t - top) for t in tops]
    inverse = 1.0 / sum(p * ref[heads : 2 * heads, :] for p, ref in zip(parts, stats))
    for b in range(4):
        scale_ref[b] = parts[b] * inverse
    delta_ref[...] = sum(p * ref[2 * heads :, :] for p, ref in zip(parts, stats)) * inverse
    rows = mate_ref.shape[0]
    seen = is_seen(MATE, seen_ref)

    @pl.when(seen)
    def _():
        next_backward(
            seen_level(MATE, seen_ref), q_ref, g_ref, mate_ref, mate_e, scale_ref.at[MATE], delta_ref, None, mate_part, gq_part, kt_ref, p_ref, ds_ref
        )

    @pl.when(jnp.logical_not(seen))
    def _():
        mate_part[...] = jnp.zeros(mate_part.shape, mate_part.dtype)
        next_backward(
            seen_level(SIDE, seen_ref), q_ref, g_ref, side_ref, side_e, scale_ref.at[SIDE], delta_ref, None,
            side_part, gq_part, kt_ref, p_ref, ds_ref,
        )


def line_kernel(seen_ref, q_ref, g_ref, kv_ref, e_ref, scale_ref, delta_ref, gq_in, part_ref, gq_ref, kt_ref, p_ref, ds_ref):
    next_backward(
        seen_level(LINE, seen_ref), q_ref, g_ref, kv_ref, e_ref, scale_ref.at[LINE], delta_ref, gq_in,
        part_ref, gq_ref, kt_ref, p_ref, ds_ref,
    )


def side_kernel(
    seen_ref, q_ref, g_ref, kv_ref, e_ref, scale_ref, delta_ref, gq_in, early_part, part_ref, gq_ref, kt_ref, p_ref, ds_ref
):
    rows = kv_ref.shape[0]
    late = is_seen(MATE, seen_ref)

    @pl.when(late)
    def _():
        next_backward(
            seen_level(SIDE, seen_ref), q_ref, g_ref, kv_ref, e_ref, scale_ref.at[SIDE], delta_ref, gq_in,
            part_ref, gq_ref, kt_ref, p_ref, ds_ref,
        )

    @pl.when(jnp.logical_not(late))
    def _():
        part_ref[...] = early_part[...]
        gq_ref[...] = gq_in[...]


def turn(h, value, buf):
    buf[:, h * value.shape[0] : (h + 1) * value.shape[0]] = jnp.transpose(value.astype(jnp.bfloat16))


def last_kernel(
    seen_ref, q_ref, g_ref, kv_ref, e_ref, scale_ref, delta_ref, gq_in, dp_ref, own_o, mate_o, line_o, side_o,
    part_ref, gq_ref, att_ref,
    kt_ref, p_ref, ds_ref, buf, att_buf, sems,
):
    factor = (kv_ref.shape[1] // 2) ** -0.5
    seen = [is_seen(role, seen_ref) for role in (MATE, LINE, SIDE)]
    for h in range(own_o.shape[0]):
        out = own_o[h] * scale_ref[OWN, h : h + 1, :]
        for taken, b, ref in zip(seen, (MATE, LINE, SIDE), (mate_o, line_o, side_o)):
            out = out + jnp.where(taken, ref[h] * scale_ref[b, h : h + 1, :], 0.0)
        turn(h, out, att_buf)
    att_copy = pltpu.make_async_copy(att_buf, att_ref, sems.at[0])
    gq_copy = pltpu.make_async_copy(buf, gq_ref, sems.at[1])
    att_copy.start()

    @pl.when(lax.axis_index("ctx") >= 0)
    def _():
        backward_queries(
            g_ref, kv_ref, e_ref, scale_ref.at[OWN], delta_ref, lambda h, v: turn(h, (gq_in[h] + v) * factor, buf),
            kt_ref, p_ref, ds_ref, dp_ref,
        )

    gq_copy.start()

    @pl.when(lax.axis_index("ctx") >= 0)
    def _():
        backward_keys(q_ref, g_ref, p_ref, ds_ref, part_ref)

    att_copy.wait()
    gq_copy.wait()


def line_add_kernel(line_ref, mate_ref, out_ref):
    out_ref[...] = (line_ref[...] + mate_ref[...].astype(jnp.float32)).astype(jnp.bfloat16)


def line_sum_kernel(own_ref, line_ref, out_ref):
    out_ref[...] = own_ref[...] + line_ref[...].astype(jnp.float32)


def side_sum_kernel(sum_ref, near_ref, far_ref, k_ref, v_ref):
    here, count = lax.axis_index("ctx"), lax.axis_size("ctx")
    dim = k_ref.shape[1]
    even = lax.rem(here, 2) == 0
    side = jnp.where(even, near_ref[...].astype(jnp.float32), far_ref[...].astype(jnp.float32))
    total = sum_ref[...] + jnp.where(even | (here + 3 < count), side, 0.0)
    k_ref[...] = total[:, :dim].astype(jnp.bfloat16)
    v_ref[...] = total[:, dim:].astype(jnp.bfloat16)


def call(name, kernel, args, outs, scratch, flops, far_in=(), far_out=(), aliases=None):
    near, far = pl.BlockSpec(memory_space=pltpu.VMEM), pl.BlockSpec(memory_space=pltpu.HBM)
    args = [pltpu.with_memory_space_constraint(a, pltpu.HBM) if i in far_in else a for i, a in enumerate(args)]
    return pl.pallas_call(
        kernel,
        name=name,
        out_shape=outs,
        in_specs=[far if i in far_in else near for i in range(len(args))],
        out_specs=[far if i in far_out else near for i in range(len(outs))],
        scratch_shapes=scratch,
        input_output_aliases=aliases or {},
        cost_estimate=pl.CostEstimate(flops=flops, bytes_accessed=0, transcendentals=0),
        compiler_params=pltpu.CompilerParams(vmem_limit_bytes=16 << 20),
    )(*args)


def three_back(count):
    to = {i: i - 3 for i in range(4, count, 2)}
    to.update({i: i + 3 for i in range(3, count - 3, 2)})
    to.update({0: 2, 1: 0, 2: 4, count - 3: count - 1, count - 1: count - 3})
    return list(to.items())


def body(queries, key_vectors, value_vectors, doc_ids, grad_out):
    rows, dim = key_vectors.shape
    heads = queries.shape[1] // dim
    count = lax.axis_size("ctx")
    to_mate = [(i, i ^ 1) for i in range(count)]
    to_line = [(i, (i + 2) % count) for i in range(count)]
    to_side = [(i, (i + 1 + 2 * (i % 2)) % count) for i in range(count)]
    flip = lambda pairs: [(b, a) for a, b in pairs]
    f32, bf16 = jnp.float32, jnp.bfloat16
    shape = jax.ShapeDtypeStruct
    e_shape, stat_shape, out_shape = shape((heads, rows, rows), bf16), shape((3 * heads, rows), f32), shape((heads, dim, rows), f32)
    pair, pair_sent = shape((rows, 2 * dim), f32), shape((rows, 2 * dim), bf16)
    wide = shape(queries.shape, bf16)
    buffer = lambda like: pltpu.VMEM(like.shape, like.dtype)
    flat = pltpu.VMEM((dim, rows), bf16)
    ahead = [pltpu.VMEM((heads, rows, rows), f32), flat]
    back = [flat, buffer(e_shape), buffer(e_shape)]
    work = heads * rows

    docs = doc_ids.reshape(-1, LANES)
    own = call(
        "pack", pack_kernel, (key_vectors, value_vectors), (pair_sent,), [pltpu.SemaphoreType.DMA((2,))], 1 << 33, (0, 1)
    )[0]
    line = lax.ppermute(own, "ctx", to_line)
    q, g = queries, grad_out
    own_e, own_stat, own_o, bias, gt, dp, seen = call(
        "own_forward", own_kernel, (docs, q, g, own),
        (e_shape, stat_shape, out_shape, shape((3, rows, rows), f32), shape((heads, dim, rows), bf16), shape((heads, rows, rows), f32),
         shape((8, LANES), jnp.int32)),
        [pltpu.VMEM((rows, rows), f32), *ahead], work,
    )
    line, own_stat = lax.optimization_barrier((line, own_stat))
    side = lax.ppermute(own, "ctx", to_side)
    mate = lax.ppermute(line, "ctx", to_mate)

    def first(name, role, kv):
        return call(
            name, lambda *refs: next_kernel(role, *refs), (seen, q, kv, bias, gt), (e_shape, stat_shape, out_shape), ahead, work
        )

    line_e, line_stat, line_o = first("line_forward", LINE, line)
    side_e, side_stat, side_o = first("side_forward", SIDE, side)
    mate_o, mate_part, early_part, gq, scales, delta = call(
        "rest_forward", rest_kernel,
        (seen, q, g, mate, side, bias, gt, own_stat, line_stat, side_stat, side_e),
        (out_shape, pair_sent, pair_sent, out_shape, shape((4, heads, rows), f32), shape((heads, rows), f32)),
        [*ahead, buffer(e_shape), buffer(stat_shape), *back],
        work,
    )
    mate_back = lax.ppermute(mate_part, "ctx", to_mate)
    line_part, gq = call(
        "line_backward", line_kernel, (seen, q, g, line, line_e, scales, delta, gq), (pair, out_shape), back, work
    )
    line_part = call("line_add", line_add_kernel, (line_part, mate_back), (pair_sent,), [], 0)[0]
    line_part, gq = lax.optimization_barrier((line_part, gq))
    side_part, gq = call(
        "side_backward", side_kernel, (seen, q, g, side, side_e, scales, delta, gq, early_part), (pair_sent, out_shape), back, work
    )
    side_far = lax.ppermute(side_part, "ctx", three_back(count))
    side_near = lax.ppermute(side_part, "ctx", to_mate)
    line_back = lax.ppermute(line_part, "ctx", flip(to_line))
    own_part, grad_query, attended = call(
        "own_backward", last_kernel, (seen, q, g, own, own_e, scales, delta, gq, dp, own_o, mate_o, line_o, side_o), (pair, wide, wide),
        [*back, buffer(wide), buffer(wide), pltpu.SemaphoreType.DMA((2,))], work, (), (1, 2),
    )
    total = call("line_sum", line_sum_kernel, (own_part, line_back), (pair,), [], work)[0]
    narrow = shape((rows, dim), bf16)
    grad_key, grad_value = call("side_sum", side_sum_kernel, (total, side_near, side_far), (narrow, narrow), [], 0)
    return attended, grad_query, grad_key, grad_value


def solution(mesh):
    return jax.shard_map(
        body,
        mesh=mesh,
        in_specs=(P("ctx", "head"), P("ctx", "head"), P("ctx", "head"), P(), P("ctx", "head")),
        out_specs=(P("ctx", "head"), P("ctx", "head"), P("ctx", "head"), P("ctx", "head")),
        check_vma=False,
    )
```
